512 devices in a mesh: row: 64 (over x, z), col: 8 (over y, core).
Axes of the slice: x: 4, y: 4, z: 16, core: 2. Of those that a mesh axis runs over, the one named last changes fastest.
Arguments:
- panel: float32 [512, 131072], P('col', 'row'), may hold values from -6 to 6
- signs: int32 [131072], P('row'), may hold values from -1 to 1, as said below
- sample_rows: int32 [8192], P('row'), may hold values from 0 to 131071, as said below
Outputs:
- sketch: float32 [512, 8192], P('col', 'row')
- gram: float32 [512, 512], P('row')
The draws below stay inside these ranges and needn't reach their ends.
Inputs may be any that keep to these rules, and one draw needn't show every extreme that they name: `sample_rows`: sorted ascending and distinct; entries b * 128 to (b + 1) * 128 - 1 lie in rows b * 2048 to (b + 1) * 2048 - 1. `signs`: each entry is -1 or 1.
All inputs are finite; a program needn't handle non-finite values.
Results may differ from the reference program's by a relative error of at most 0.00013.
Values sent between devices are 32-bit elements; how exact they have to be, the bound alone decides.
A program may use at most 64 MiB of HBM per device.

```python
import jax
import jax.numpy as jnp
from jax import lax

COLS = 512
ROWS_DEV = 2048
SAMP_DEV = 128
ROWS = 131072
SAMPLES = 8192
N_ROW = 64


def draw_signs(key, part):
    key = jax.random.fold_in(key, 11)
    return (2 * jax.random.randint(key, (ROWS,), 0, 2, dtype=jnp.int32) - 1).astype(jnp.int32)


def block_samples(key):
    inside = jax.random.permutation(key, ROWS_DEV - 2)[:SAMP_DEV - 2].astype(jnp.int32) + 1
    first = jnp.zeros((1,), jnp.int32)
    last = jnp.full((1,), ROWS_DEV - 1, jnp.int32)
    return jnp.sort(jnp.concatenate([first, inside, last])).astype(jnp.int32)


def draw_sample_rows(key, part):
    key = jax.random.fold_in(key, 23)
    block_count = ROWS // ROWS_DEV
    keys = jax.random.split(key, block_count)
    offsets = jax.vmap(block_samples)(keys)
    starts = (jnp.arange(block_count, dtype=jnp.int32) * ROWS_DEV)[:, None]
    return (offsets + starts).reshape(SAMPLES).astype(jnp.int32)


def block_scale(rng, shape, shards, smallest, high):
    level = 1.0
    for dim, blocks in shards:
        draws = jax.random.uniform(jax.random.fold_in(jax.random.fold_in(rng, 6), dim), (blocks,), jnp.float32, smallest / len(shards), high / len(shards))
        level = level * jnp.repeat(jnp.exp(draws), shape[dim] // blocks).reshape((-1,) + (1,) * (len(shape) - 1 - dim))
    return level


def centred(stream_key, dims, width, most, cuts=(), kind=jnp.bfloat16):
    entries = jax.random.normal(stream_key, dims, jnp.float32) * width
    if len(cuts) > 0:
        entries = block_scale(stream_key, dims, cuts, -0.22, 0.18) * entries
    return jnp.clip(entries, min=-most, max=most).astype(kind)


def setup_inputs(seed: int = 0) -> dict:
    key_of = jax.random.split(jax.random.key(seed), 4)
    panel = centred(key_of[0], (COLS, ROWS), 1.0, 6.0, ((0, 8), (1, 64)), jnp.float32)
    signs = draw_signs(jax.random.fold_in(key_of[3], 71), 0)
    sample_rows = draw_sample_rows(jax.random.fold_in(key_of[3], 71), 0)
    return dict(panel=panel, signs=signs, sample_rows=sample_rows)


def hadamard_table(order):
    first = jnp.arange(order, dtype=jnp.int32)[:, None]
    second = jnp.arange(order, dtype=jnp.int32)[None, :]
    parity = jnp.zeros((order, order), jnp.int32)
    for level in range(order.bit_length() - 1):
        parity = parity + jnp.bitwise_and(jnp.right_shift(first, level), 1) * jnp.bitwise_and(jnp.right_shift(second, level), 1)
    return (1 - 2 * (parity % 2)).astype(jnp.float32)

def reference(panel, signs, sample_rows):
    outer = hadamard_table(N_ROW)
    middle = hadamard_table(ROWS_DEV // 128)
    inner = hadamard_table(128)
    scale = 1.0 / jnp.sqrt(jnp.float32(ROWS))
    high = lax.Precision.HIGHEST

    def mix_block(block):
        signed = block * signs[None, :].astype(jnp.float32)
        shaped = signed.reshape(block.shape[0], N_ROW, ROWS_DEV // 128, 128)
        shaped = jnp.einsum('cdab,be->cdae', shaped, inner, precision=high)
        shaped = jnp.einsum('fa,cdab->cdfb', middle, shaped, precision=high)
        shaped = jnp.einsum('gd,cdab->cgab', outer, shaped, precision=high)
        mixed = shaped.reshape(block.shape[0], ROWS) * scale
        return jnp.take(mixed, sample_rows, axis=1)
    blocks = panel.reshape(COLS // 64, 64, ROWS)
    sketch = lax.map(mix_block, blocks).reshape(COLS, SAMPLES)
    gram = jnp.dot(sketch, sketch.T, precision=high, preferred_element_type=jnp.float32) / SAMPLES
    return (sketch, gram)
```

```python
import functools

import jax
import jax.numpy as jnp
from jax import lax
from jax.experimental import pallas as pl
from jax.experimental.pallas import tpu as pltpu
from jax.sharding import PartitionSpec as P

MESH = pl.DeviceIdType.MESH
LANES = 128


def parity_sign(bits):
    bits = bits ^ (bits >> 4)
    bits = bits ^ (bits >> 2)
    bits = bits ^ (bits >> 1)
    return (1 - 2 * (bits & 1)).astype(jnp.float32)


def split_hi_lo(value):
    hi = value.astype(jnp.bfloat16)
    return hi, (value - hi.astype(jnp.float32)).astype(jnp.bfloat16)


def butterfly(blocks):
    blocks = list(blocks)
    step = 1
    while step < len(blocks):
        for first in range(len(blocks)):
            if not first & step:
                low, high = blocks[first], blocks[first + step]
                blocks[first], blocks[first + step] = low + high, low - high
        step *= 2
    return blocks


def kernel(
    dims, panel_ref, signs_ref, samp_ref, sketch_ref, gram_ref,
    panel, xs, xr, samples, had, mask, mixed, send_dn, send_up, recv_dn, recv_up,
    own, rows, tile, tile_in, final,
    panel_sem, sx_send, sx_recv, sz_send, sz_recv, x_send, x_recv,
    dn_send, dn_recv, up_send, up_recv, own_send, own_recv, row_send, row_recv,
    gz_send, gz_recv, gc_send, gc_recv,
):
    nx, nz, ny, nc, parts = dims
    width, length = panel.shape
    block = width // nx
    groups = length // LANES
    down_steps, up_steps = nz // 2, nz // 2 - 1
    per_part = nx // parts
    row, col = lax.axis_index("row"), lax.axis_index("col")
    x, z = row // nz, lax.rem(row, nz)
    y, core = col // nc, lax.rem(col, nc)

    def at(px, pz, pc):
        return {"row": px * nz + pz, "col": pc}

    def x_peer(k):
        return lax.rem(x + k, nx)

    def z_peer(k):
        return lax.rem(z + k, nz)

    def copy(src, dst, send, recv, where):
        return pltpu.make_async_remote_copy(
            src_ref=src, dst_ref=dst, send_sem=send, recv_sem=recv,
            device_id=where, device_id_type=MESH,
        )

    load = pltpu.make_async_copy(panel_ref, panel, panel_sem)
    load.start()

    barrier = pltpu.get_barrier_semaphore()

    def greet(where):
        pl.semaphore_signal(barrier, inc=1, device_id=where, device_id_type=MESH)

    for k in range(1, nx):
        greet(at(x_peer(k), z, col))
    for k in range(1, nz):
        greet(at(x, z_peer(k), col))
    for k in range(1, ny * nc):
        greet(at(x, z, lax.rem(col + k, ny * nc)))
    for k in range(nx):
        for dc in range(nc):
            where = at(x_peer(k), z, x * nc + lax.rem(core + dc, nc))
            if k == 0 and dc == 0:
                @pl.when(x != y)
                def _():
                    greet(where)
            else:
                greet(where)

    samples[z, x] = samp_ref[...]
    load.wait()
    for jh in range(groups):
        lanes = slice(jh * LANES, (jh + 1) * LANES)
        sign = signs_ref[jh : jh + 1, :].astype(jnp.float32)
        signed = panel[:, lanes] * sign
        for d in range(nx):
            xs[d, jh * block : (jh + 1) * block, :] = signed[d * block : (d + 1) * block]
    greeted = nx - 1 + nz - 1 + ny * nc - 1 + nx * nc
    pl.semaphore_wait(barrier, greeted - jnp.where(x == y, 1, 0))

    sx = [copy(samples.at[z, x], samples.at[z, x], sx_send.at[k], sx_recv.at[k], at(x_peer(k), z, col)) for k in range(1, nx)]
    for c in sx:
        c.start()
    xc = [copy(xs.at[x_peer(k)], xr.at[x], x_send.at[k], x_recv.at[k], at(x_peer(k), z, col)) for k in range(1, nx)]
    for c in xc:
        c.start()
    xr[x] = xs[x]
    for k in range(1, nx):
        copy(samples.at[z, x], samples.at[z, x_peer(nx - k)], sx_send.at[k], sx_recv.at[k], at(x_peer(k), z, col)).wait_recv()

    def sz(k):
        return copy(samples.at[z], samples.at[z], sz_send.at[k], sz_recv.at[k], at(x, z_peer(k), col))

    @pl.loop(1, nz)
    def _(k):
        sz(k).start()

    lane_bits = lax.broadcasted_iota(jnp.int32, (8, LANES), 0)
    high_bits = lax.broadcasted_iota(jnp.int32, (groups, LANES), 0)

    def tables(t):
        both = z * 0
        for b in range(nz.bit_length() - 1):
            both = both + lax.rem(z // (1 << b), 2) * lax.rem(t // (1 << b), 2)
        z_sign = (1 - 2 * lax.rem(both, 2)).astype(jnp.float32)
        for xx in range(nx):
            place = samples[t, xx]
            base = parity_sign(lane_bits & place)
            wide = [base]
            for b in range(3, 7):
                factor = (1 - 2 * ((place >> b) & 1)).astype(jnp.float32)
                wide = wide + [w * factor for w in wide]
            had[t, xx] = jnp.concatenate(wide, axis=0).astype(jnp.bfloat16)
            mask[t, xx] = parity_sign(high_bits & (place >> 7)) * z_sign

    tables(z)

    @pl.loop(1, nz)
    def _(k):
        src = z_peer(nz - k)
        copy(samples.at[src], samples.at[src], sz_send.at[k], sz_recv.at[k], at(x, z_peer(k), col)).wait_recv()
        tables(src)

    for k in range(1, nx):
        copy(xs.at[x_peer(k)], xr.at[x_peer(nx - k)], x_send.at[k], x_recv.at[k], at(x_peer(k), z, col)).wait_recv()
    for jh in range(groups):
        part = slice(jh * block, (jh + 1) * block)
        for xx, value in enumerate(butterfly([xr[d, part] for d in range(nx)])):
            hi, lo = split_hi_lo(value)
            mixed[xx, part, :LANES] = hi
            mixed[xx, part, LANES:] = lo

    def dn(k, p):
        span = pl.ds(p * per_part, per_part)
        return copy(send_dn.at[k, span], recv_dn.at[k, span], dn_send.at[k, p], dn_recv.at[k, p], at(x, z_peer(nz - 1), col))

    def up(k, p):
        span = pl.ds(p * per_part, per_part)
        return copy(send_up.at[k, span], recv_up.at[k, span], up_send.at[k, p], up_recv.at[k, p], at(x, z_peer(1), col))

    @pl.loop(0, down_steps)
    def _(k):
        t_dn = lax.rem(z + nz - down_steps + k, nz)
        t_up = lax.rem(z + up_steps - k, nz)
        for xx in range(nx):
            table = jnp.concatenate([had[t_dn, xx], had[t_up, xx]], axis=1)
            table = jnp.concatenate([table, table], axis=0)
            product = jnp.dot(mixed[xx], table, preferred_element_type=jnp.float32)
            signs_dn, signs_up = mask[t_dn, xx], mask[t_up, xx]
            total_dn = total_up = None
            for jh in range(groups):
                part = product[jh * block : (jh + 1) * block]
                term_dn = part[:, :LANES] * signs_dn[jh : jh + 1]
                term_up = part[:, LANES:] * signs_up[jh : jh + 1]
                total_dn = term_dn if jh == 0 else total_dn + term_dn
                total_up = term_up if jh == 0 else total_up + term_up
            send_dn[k, xx] = total_dn
            send_up[k, xx] = total_up
        for p in range(parts):
            span = pl.ds(p * per_part, per_part)

            @pl.when(k > 0)
            def _():
                dn(k - 1, p).wait_recv()
                send_dn[k, span] = send_dn[k, span] + recv_dn[k - 1, span]

            dn(k, p).start()

            @pl.when(k > 0)
            def _():
                up(k - 1, p).wait_recv()
                send_up[k, span] = send_up[k, span] + recv_up[k - 1, span]

            @pl.when(k < up_steps)
            def _():
                up(k, p).start()

    scale = 1.0 / jnp.sqrt(jnp.float32(length * nx * nz))
    for p in range(parts):
        span = pl.ds(p * per_part, per_part)
        dn(down_steps - 1, p).wait_recv()
        own[x, span] = (send_up[up_steps, span] + recv_dn[down_steps - 1, span]) * scale

    def own_copy(k):
        return copy(own.at[x], own.at[x], own_send.at[k], own_recv.at[k], at(x_peer(k), z, col))

    def row_copy(dy, dc):
        where = at(y, z, lax.rem(y + dy, ny) * nc + lax.rem(core + dc, nc))
        return copy(own.at[x], rows.at[core, x], row_send.at[dy, dc], row_recv.at[dc, x], where)

    for k in range(1, nx):
        own_copy(k).start()
    for dy in range(ny):
        for dc in range(nc):
            if dy == 0 and dc == 0:
                @pl.when(x != y)
                def _():
                    row_copy(0, 0).start()

                @pl.when(x == y)
                def _():
                    rows[core, x] = own[x]
            else:
                row_copy(dy, dc).start()
    for k in range(1, nx):
        src = x_peer(nx - k)
        copy(own.at[x], own.at[src], own_send.at[k], own_recv.at[k], at(x_peer(k), z, col)).wait_recv()
    for b in range(nx):
        sketch_ref[b * block : (b + 1) * block, :] = own[b, x]
    for k in range(nx):
        for dc in range(nc):
            src = x_peer(k)
            incoming = copy(
                own.at[x], rows.at[lax.rem(core + nc - dc, nc), src], row_send.at[0, dc], row_recv.at[dc, src],
                at(y, z, lax.rem(y + 1, ny) * nc + core),
            )
            if k == 0 and dc == 0:
                @pl.when(x != y)
                def _():
                    incoming.wait_recv()
            else:
                incoming.wait_recv()

    total = None
    blank = jnp.zeros((width, LANES), jnp.float32)
    for b in range(nx):
        left = jnp.concatenate([rows[c, d, b] for c in range(nc) for d in range(nx)], axis=0)
        right = jnp.concatenate([own[d, b] for d in range(nx)], axis=0)
        first = jnp.where(core == 0, right, blank)
        right = jnp.concatenate([first, right - first], axis=0)
        left_hi, left_lo = split_hi_lo(left)
        right_hi, right_lo = split_hi_lo(right)
        term = lax.dot_general(
            jnp.concatenate([left_hi, left_hi, left_lo], axis=1),
            jnp.concatenate([right_hi, right_lo, right_hi], axis=1),
            (((1,), (1,)), ((), ())),
            preferred_element_type=jnp.float32,
        )
        total = term if b == 0 else total + term
    tile[...] = total.reshape(tile.shape)

    def gz(k):
        return copy(tile.at[z_peer(k)], tile_in.at[k], gz_send.at[k], gz_recv.at[k], at(x, z_peer(k), col))

    @pl.loop(1, nz)
    def _(k):
        gz(k).start()

    total = tile[z]
    for k in range(1, nz):
        gz(k).wait_recv()
        total = total + tile_in[k]
    final[col] = total * (1.0 / (LANES * nx * nz))

    def gc(k):
        return copy(final.at[col], final.at[col], gc_send.at[k], gc_recv.at[k], at(x, z, lax.rem(col + k, ny * nc)))

    for k in range(1, ny * nc):
        gc(k).start()
    for k in range(1, ny * nc):
        src = lax.rem(col + ny * nc - k, ny * nc)
        copy(final.at[col], final.at[src], gc_send.at[k], gc_recv.at[k], at(x, z, lax.rem(col + k, ny * nc))).wait_recv()
    for b in range(ny):
        both = final[b * nc]
        for c in range(1, nc):
            both = both + final[b * nc + c]
        gram_ref[:, b * LANES : (b + 1) * LANES] = both

    for c in sx + xc:
        c.wait_send()

    @pl.loop(1, nz)
    def _(k):
        sz(k).wait_send()
        gz(k).wait_send()

    @pl.loop(0, down_steps)
    def _(k):
        for p in range(parts):
            dn(k, p).wait_send()

            @pl.when(k < up_steps)
            def _():
                up(k, p).wait_send()

    for k in range(1, nx):
        own_copy(k).wait_send()
    for dy in range(ny):
        for dc in range(nc):
            if dy == 0 and dc == 0:
                @pl.when(x != y)
                def _():
                    row_copy(0, 0).wait_send()
            else:
                row_copy(dy, dc).wait_send()
    for k in range(1, ny * nc):
        gc(k).wait_send()


def per_device(dims, panel, signs, sample_rows):
    nx, nz, ny, nc, parts = dims
    width, length = panel.shape
    block, groups = width // nx, length // LANES
    gram_rows = width * nc // nz
    place = jnp.bitwise_and(sample_rows, length - 1).reshape(1, LANES)
    f32, bf16 = jnp.float32, jnp.bfloat16
    vmem, dma = pltpu.VMEM, pltpu.SemaphoreType.DMA
    down, up = nz // 2, nz // 2 - 1
    return pl.pallas_call(
        functools.partial(kernel, dims),
        out_shape=(
            jax.ShapeDtypeStruct((width, LANES), f32),
            jax.ShapeDtypeStruct((gram_rows, width * ny * nc), f32),
        ),
        in_specs=[
            pl.BlockSpec(memory_space=pl.ANY),
            pl.BlockSpec(memory_space=vmem),
            pl.BlockSpec(memory_space=vmem),
        ],
        out_specs=(pl.BlockSpec(memory_space=vmem), pl.BlockSpec(memory_space=vmem)),
        scratch_shapes=[
            vmem((width, length), f32),
            vmem((nx, groups * block, LANES), f32),
            vmem((nx, groups * block, LANES), f32),
            vmem((nz, nx, 1, LANES), jnp.int32),
            vmem((nz, nx, LANES, LANES), bf16),
            vmem((nz, nx, groups, LANES), f32),
            vmem((nx, groups * block, 2 * LANES), bf16),
            vmem((down, nx, block, LANES), f32),
            vmem((down, nx, block, LANES), f32),
            vmem((down, nx, block, LANES), f32),
            vmem((down, nx, block, LANES), f32),
            vmem((nx, nx, block, LANES), f32),
            vmem((nc, nx, nx, block, LANES), f32),
            vmem((nz, gram_rows, LANES), f32),
            vmem((nz, gram_rows, LANES), f32),
            vmem((ny * nc, gram_rows, LANES), f32),
            dma, dma((nx,)), dma((nx,)), dma((nz,)), dma((nz,)), dma((nx,)), dma((nx,)),
            dma((down, parts)), dma((down, parts)), dma((down, parts)), dma((down, parts)),
            dma((nx,)), dma((nx,)), dma((ny, nc)), dma((nc, nx)),
            dma((nz,)), dma((nz,)), dma((ny * nc,)), dma((ny * nc,)),
        ],
        compiler_params=pltpu.CompilerParams(
            collective_id=0, has_side_effects=True, vmem_limit_bytes=32 * 1024 * 1024
        ),
        cost_estimate=pl.CostEstimate(flops=1 << 30, bytes_accessed=1 << 20, transcendentals=0),
    )(panel, signs.reshape(groups, LANES), place)


def build(mesh, dims):
    return jax.shard_map(
        functools.partial(per_device, dims),
        mesh=mesh,
        in_specs=(P("col", "row"), P("row"), P("row")),
        out_specs=(P("col", "row"), P("row", None)),
        check_vma=False,
    )


def solution(mesh):
    return build(mesh, (4, 16, 4, 2, 2))
```

```python
import functools

import jax
import jax.numpy as jnp
from jax import lax
from jax.experimental import pallas as pl
from jax.experimental.pallas import tpu as pltpu
from jax.sharding import PartitionSpec as P

MESH = pl.DeviceIdType.MESH
LANES = 128


def parity_sign(bits):
    bits = bits ^ (bits >> 4)
    bits = bits ^ (bits >> 2)
    bits = bits ^ (bits >> 1)
    return (1 - 2 * (bits & 1)).astype(jnp.float32)


def split_hi_lo(value):
    hi = value.astype(jnp.bfloat16)
    return hi, (value - hi.astype(jnp.float32)).astype(jnp.bfloat16)


def butterfly(blocks):
    blocks = list(blocks)
    step = 1
    while step < len(blocks):
        for first in range(len(blocks)):
            if not first & step:
                low, high = blocks[first], blocks[first + step]
                blocks[first], blocks[first + step] = low + high, low - high
        step *= 2
    return blocks


def kernel(
    dims, panel_ref, signs_ref, samp_ref, sketch_ref, gram_ref,
    panel, signs, samp, xs, xr, samples, had, mask, mixed, part_out, part_in,
    own, rows, tile, tile_in, final, gathered,
    load_sem, s1_send, s1_recv, s2_send, s2_recv, x_send, x_recv, p_send, p_recv,
    own_send, own_recv, row_send, row_recv, t_send, t_recv, f_send, f_recv,
):
    nx, nz, ny, nc = dims
    width, length = panel.shape
    near, far, cols = 2 * nx, nz // 2, ny * nc
    turns = nz // near
    block = width // near
    groups = length // LANES
    row, col = lax.axis_index("row"), lax.axis_index("col")
    x, z = row // nz, lax.rem(row, nz)
    zh, zl = z // 2, lax.rem(z, 2)
    g = 2 * x + zl

    def copy(src, dst, send, recv, where):
        return pltpu.make_async_remote_copy(
            src_ref=src, dst_ref=dst, send_sem=send, recv_sem=recv,
            device_id=where, device_id_type=MESH,
        )

    def near_id(k):
        return lax.rem(g + k, near)

    def near_at(k):
        other = near_id(k)
        return {"row": (other // 2) * nz + 2 * zh + lax.rem(other, 2), "col": col}

    def far_id(k):
        return lax.rem(zh + k, far)

    def far_at(k):
        return {"row": x * nz + 2 * far_id(k) + zl, "col": col}

    def col_id(k):
        return lax.rem(col + k, cols)

    def col_at(k):
        return {"row": row, "col": col_id(k)}

    hub = lax.rem(zh, nx)

    loads = [
        pltpu.make_async_copy(src, dst, load_sem.at[i])
        for i, (src, dst) in enumerate([(samp_ref, samp), (signs_ref, signs), (panel_ref, panel)])
    ]
    for c in loads:
        c.start()

    barrier = pltpu.get_barrier_semaphore()

    def greet(where):
        pl.semaphore_signal(barrier, inc=1, device_id=where, device_id_type=MESH)

    for k in range(1, near):
        greet(near_at(k))
    for k in range(1, far):
        greet(far_at(k))
    for k in range(1, cols):
        greet(col_at(k))

    @pl.when(x != hub)
    def _():
        for k in range(cols):
            greet({"row": hub * nz + z, "col": col_id(k)})

    for c in loads:
        c.wait()
    samples[zh, g] = samp[...] & (length - 1)
    for jh in range(groups):
        sign = signs[jh : jh + 1, :].astype(jnp.float32)
        signed = panel[:, jh * LANES : (jh + 1) * LANES] * sign
        for d in range(near):
            xs[d, jh * block : (jh + 1) * block, :] = signed[d * block : (d + 1) * block]
    greeted = near - 1 + far - 1 + cols - 1
    pl.semaphore_wait(barrier, greeted + jnp.where(x == hub, (nx - 1) * cols, 0))
    def s1(k):
        return copy(samples.at[zh, g], samples.at[zh, g], s1_send.at[k], s1_recv.at[k], near_at(k))

    def s2(k):
        return copy(samples.at[zh], samples.at[zh], s2_send.at[k], s2_recv.at[k], far_at(k))

    def xc(k):
        return copy(xs.at[near_id(k)], xr.at[g], x_send.at[k], x_recv.at[k], near_at(k))

    for k in range(1, near):
        s1(k).start()
    for k in range(1, near):
        xc(k).start()
    xr[g] = xs[g]
    for k in range(1, near):
        src = near_id(near - k)
        copy(samples.at[zh, g], samples.at[zh, src], s1_send.at[k], s1_recv.at[k], near_at(k)).wait_recv()
    for k in range(1, far):
        s2(k).start()

    lane_bits = lax.broadcasted_iota(jnp.int32, (8, LANES), 0)
    high_bits = lax.broadcasted_iota(jnp.int32, (groups, LANES), 0)

    def tables(t):
        both = zh * 0
        for b in range(far.bit_length() - 1):
            both = both + lax.rem(zh // (1 << b), 2) * lax.rem(t // (1 << b), 2)
        far_sign = (1 - 2 * lax.rem(both, 2)).astype(jnp.float32)

        @pl.loop(0, near)
        def _(i):
            place = samples[t, i]
            wide = [parity_sign(lane_bits & place)]
            for b in range(3, 7):
                factor = (1 - 2 * ((place >> b) & 1)).astype(jnp.float32)
                wide = wide + [w * factor for w in wide]
            had[t, i] = jnp.concatenate(wide, axis=0).astype(jnp.bfloat16)
            mask[t, i] = parity_sign(high_bits & (place >> 7)) * far_sign

    tables(zh)
    for k in range(1, far):
        src = far_id(far - k)
        copy(samples.at[zh], samples.at[src], s2_send.at[k], s2_recv.at[k], far_at(k)).wait_recv()
        tables(src)

    for k in range(1, near):
        src = near_id(near - k)
        copy(xs.at[g], xr.at[src], x_send.at[k], x_recv.at[k], near_at(k)).wait_recv()
    for jh in range(groups):
        part = slice(jh * block, (jh + 1) * block)
        for i, value in enumerate(butterfly([xr[d, part] for d in range(near)])):
            hi, lo = split_hi_lo(value)
            mixed[i, part, :LANES] = hi
            mixed[i, part, LANES:] = lo
    def pc(k):
        return copy(part_out.at[k], part_in.at[k], p_send.at[k], p_recv.at[k], far_at(k))

    order = sorted(range(far), key=lambda k: -min(k, far - k))
    for first, second in zip(order[::2], order[1::2]):
        targets = (far_id(first), far_id(second))

        @pl.loop(0, near)
        def _(i):
            table = jnp.concatenate([had[t, i] for t in targets], axis=1)
            table = jnp.concatenate([table, table], axis=0)
            product = jnp.dot(mixed[i], table, preferred_element_type=jnp.float32)
            for n, (k, t) in enumerate(zip((first, second), targets)):
                signs_t = mask[t, i]
                total = None
                for jh in range(groups):
                    term = product[jh * block : (jh + 1) * block, n * LANES : (n + 1) * LANES] * signs_t[jh : jh + 1]
                    total = term if jh == 0 else total + term
                part_out[k, i] = total

        for k in (first, second):
            if k:
                pc(k).start()
    total = part_out[0]
    for k in reversed([k for k in order if k]):
        pc(k).wait_recv()
        total = total + part_in[k]
    own[g] = total * (1.0 / jnp.sqrt(jnp.float32(length * nx * nz)))
    def own_copy(k):
        return copy(own.at[g], own.at[g], own_send.at[k], own_recv.at[k], near_at(k))

    def row_copy(k):
        return copy(own.at[g], rows.at[col], row_send.at[k], row_recv.at[k], col_at(k))

    for k in range(1, cols):
        row_copy(k).start()
    for k in range(1, near):
        own_copy(k).start()
    rows[col] = own[g]
    for k in range(1, cols):
        src = col_id(cols - k)
        copy(own.at[g], rows.at[src], row_send.at[k], row_recv.at[k], col_at(k)).wait_recv()
    for k in range(1, near):
        src = near_id(near - k)
        copy(own.at[g], own.at[src], own_send.at[k], own_recv.at[k], near_at(k)).wait_recv()
    total = None
    blank = jnp.zeros((width, LANES), jnp.float32)
    odd = lax.rem(col, 2)
    for b in range(near):
        left = jnp.concatenate([rows[turns * d + m, b] for m in range(turns) for d in range(nx)], axis=0)
        right = jnp.concatenate([own[d, b] for d in range(near)], axis=0)
        first = jnp.where(odd == 0, right, blank)
        right = jnp.concatenate([first, right - first], axis=0)
        left_hi, left_lo = split_hi_lo(left)
        right_hi, right_lo = split_hi_lo(right)
        term = lax.dot_general(
            jnp.concatenate([left_hi, left_hi, left_lo], axis=1),
            jnp.concatenate([right_hi, right_lo, right_hi], axis=1),
            (((1,), (1,)), ((), ())),
            preferred_element_type=jnp.float32,
        )
        total = term if b == 0 else total + term
    tile[...] = total.reshape(tile.shape)

    def tc(m):
        target = nx * m + x
        return copy(
            tile.at[m], tile_in.at[zh], t_send.at[m], t_recv.at[zh], {"row": x * nz + 2 * target + zl, "col": col}
        )

    for m in range(turns):
        @pl.when(zh != nx * m + x)
        def _():
            tc(m).start()
    for d in range(near):
        sketch_ref[d * block : (d + 1) * block, :] = own[d, g]

    def fc(kx, kc):
        dest = lax.rem(x + kx, nx)
        return copy(
            final.at[dest], gathered.at[col], f_send.at[kx, kc], f_recv.at[col], {"row": dest * nz + z, "col": col_id(kc)}
        )

    @pl.when(x == hub)
    def _():
        total = tile[zh // nx]
        for k in range(1, far):
            src = far_id(far - k)
            copy(tile.at[0], tile_in.at[src], t_send.at[0], t_recv.at[src], far_at(k)).wait_recv()
            total = total + tile_in[src]
        final[...] = total * (1.0 / (LANES * nx * nz))
        gathered[col] = final[x]
        for kx in range(nx - 1, -1, -1):
            for kc in range(cols):
                if kx or kc:
                    fc(kx, kc).start()
    def incoming(k):
        src = col_id(k)
        return copy(final.at[0], gathered.at[src], f_send.at[0, k], f_recv.at[src], col_at(k))

    for k in range(1, cols):
        incoming(k).wait_recv()

    @pl.when(x != hub)
    def _():
        copy(final.at[0], gathered.at[col], f_send.at[0, 1], f_recv.at[col], col_at(1)).wait_recv()

    for b in range(cols // 2):
        gram_ref[:, b * LANES : (b + 1) * LANES] = gathered[2 * b] + gathered[2 * b + 1]

    for k in range(1, near):
        s1(k).wait_send()
        xc(k).wait_send()
        own_copy(k).wait_send()
    for k in range(1, far):
        s2(k).wait_send()
        pc(k).wait_send()
    for k in range(1, cols):
        row_copy(k).wait_send()
    for m in range(turns):
        @pl.when(zh != nx * m + x)
        def _():
            tc(m).wait_send()

    @pl.when(x == hub)
    def _():
        for kx in range(nx):
            for kc in range(cols):
                if kx or kc:
                    fc(kx, kc).wait_send()


def per_device(dims, panel, signs, sample_rows):
    nx, nz, ny, nc = dims
    near, far, cols = 2 * nx, nz // 2, ny * nc
    turns = nz // near
    width, length = panel.shape
    block, groups = width // near, length // LANES
    f32, bf16, i32 = jnp.float32, jnp.bfloat16, jnp.int32
    vmem, dma = pltpu.VMEM, pltpu.SemaphoreType.DMA
    return pl.pallas_call(
        functools.partial(kernel, dims),
        out_shape=(
            jax.ShapeDtypeStruct((width, LANES), f32),
            jax.ShapeDtypeStruct((block, width * cols), f32),
        ),
        in_specs=[pl.BlockSpec(memory_space=pl.ANY)] * 3,
        out_specs=(pl.BlockSpec(memory_space=vmem), pl.BlockSpec(memory_space=vmem)),
        scratch_shapes=[
            vmem((width, length), f32),
            vmem((groups, LANES), i32),
            vmem((1, LANES), i32),
            vmem((near, groups * block, LANES), f32),
            vmem((near, groups * block, LANES), f32),
            vmem((far, near, 1, LANES), i32),
            vmem((far, near, LANES, LANES), bf16),
            vmem((far, near, groups, LANES), f32),
            vmem((near, groups * block, 2 * LANES), bf16),
            vmem((far, near, block, LANES), f32),
            vmem((far, near, block, LANES), f32),
            vmem((near, near, block, LANES), f32),
            vmem((cols, near, block, LANES), f32),
            vmem((turns, nx, block, LANES), f32),
            vmem((far, nx, block, LANES), f32),
            vmem((nx, block, LANES), f32),
            vmem((cols, block, LANES), f32),
            dma((3,)), dma((near,)), dma((near,)), dma((far,)), dma((far,)), dma((near,)), dma((near,)),
            dma((far,)), dma((far,)), dma((near,)), dma((near,)), dma((cols,)), dma((cols,)),
            dma((turns,)), dma((far,)), dma((nx, cols)), dma((cols,)),
        ],
        compiler_params=pltpu.CompilerParams(
            collective_id=0, has_side_effects=True, vmem_limit_bytes=60 * 1024 * 1024
        ),
        cost_estimate=pl.CostEstimate(flops=1 << 30, bytes_accessed=1 << 20, transcendentals=0),
    )(panel, signs.reshape(groups, LANES), sample_rows.reshape(1, LANES))


def build(mesh, dims):
    return jax.shard_map(
        functools.partial(per_device, dims),
        mesh=mesh,
        in_specs=(P("col", "row"), P("row"), P("row")),
        out_specs=(P("col", "row"), P("row", None)),
        check_vma=False,
    )


def solution(mesh):
    return build(mesh, (4, 16, 4, 2))
```

```python
import functools

import jax
import jax.numpy as jnp
from jax import lax
from jax.experimental import pallas as pl
from jax.experimental.pallas import tpu as pltpu
from jax.sharding import PartitionSpec as P

MESH = pl.DeviceIdType.MESH
LANES = 128


def parity_sign(bits):
    bits = bits ^ (bits >> 4)
    bits = bits ^ (bits >> 2)
    bits = bits ^ (bits >> 1)
    return (1 - 2 * (bits & 1)).astype(jnp.float32)


def split_hi_lo(value):
    hi = value.astype(jnp.bfloat16)
    return hi, (value - hi.astype(jnp.float32)).astype(jnp.bfloat16)


def butterfly(blocks):
    blocks = list(blocks)
    step = 1
    while step < len(blocks):
        for first in range(len(blocks)):
            if not first & step:
                low, high = blocks[first], blocks[first + step]
                blocks[first], blocks[first + step] = low + high, low - high
        step *= 2
    return blocks


def kernel(
    dims, panel_ref, signs_ref, samp_ref, sketch_ref, gram_ref,
    panel, signs, samp, xs, xr, samples, had, mask, mixed, part_out, part_in,
    own, rows, tile, tile_in, final, gathered,
    load_sem, s_send, s_recv, pass_send, pass_recv, x_send, x_recv, p_send, p_recv,
    own_send, own_recv, row_send, row_recv, t_send, t_recv, f_send, f_recv,
):
    nx, nz, ny, nc = dims
    width, length = panel.shape
    near, far, cols = 2 * nx, nz // 2, ny * nc
    turns = nz // near
    block = width // near
    groups = length // LANES
    row, col = lax.axis_index("row"), lax.axis_index("col")
    x, z = row // nz, lax.rem(row, nz)
    zh, zl = z // 2, lax.rem(z, 2)
    g = 2 * x + zl

    def copy(src, dst, send, recv, where):
        return pltpu.make_async_remote_copy(
            src_ref=src, dst_ref=dst, send_sem=send, recv_sem=recv,
            device_id=where, device_id_type=MESH,
        )

    def near_id(k):
        return lax.rem(g + k, near)

    def near_at(k):
        other = near_id(k)
        return {"row": (other // 2) * nz + 2 * zh + lax.rem(other, 2), "col": col}

    def far_id(k):
        return lax.rem(zh + k, far)

    def far_at(k):
        return {"row": x * nz + 2 * far_id(k) + zl, "col": col}

    def col_id(k):
        return lax.rem(col + k, cols)

    def col_at(k):
        return {"row": row, "col": col_id(k)}

    hub = lax.rem(zh, nx)

    slots = sorted(range(far), key=lambda k: (min(k, far - k), k))
    close = 1 + sum(0 < min(k, far - k) <= far // 4 for k in slots)
    batches = [(0, 1), (1, close), (close, far)]

    loads = [
        pltpu.make_async_copy(src, dst, load_sem.at[i])
        for i, (src, dst) in enumerate([(samp_ref, samp), (signs_ref, signs), (panel_ref, panel)])
    ]
    for c in loads:
        c.start()

    barrier = pltpu.get_barrier_semaphore()

    def greet(where):
        pl.semaphore_signal(barrier, inc=1, device_id=where, device_id_type=MESH)

    for k in reversed(slots[1:]):
        greet(far_at(k))
    for k in range(1, near):
        greet(near_at(k))
    for k in range(1, cols):
        greet(col_at(k))

    for c in loads:
        c.wait()
    samples[g, 0] = samp[...]
    for jh in range(groups):
        sign = signs[jh : jh + 1, :].astype(jnp.float32)
        signed = panel[:, jh * LANES : (jh + 1) * LANES] * sign
        for d in range(near):
            xs[d, jh * block : (jh + 1) * block, :] = signed[d * block : (d + 1) * block]
    pl.semaphore_wait(barrier, near - 1 + far - 1 + cols - 1)
    def sc(k):
        return copy(samp, samples.at[g, slots.index((far - k) % far)], s_send.at[k], s_recv.at[k], far_at(k))

    def sc_wait(k):
        copy(samp, samples.at[g, slots.index(k)], s_send.at[k], s_recv.at[far - k], far_at(k)).wait_recv()

    def hand_on(b, k, whose):
        first, end = batches[b]
        span = samples.at[whose, pl.ds(first, end - first)]
        return copy(span, span, pass_send.at[b, k], pass_recv.at[b, k], near_at(k))

    def xc(k):
        return copy(xs.at[near_id(k)], xr.at[g], x_send.at[k], x_recv.at[k], near_at(k))

    for k in reversed(slots[1:]):
        sc(k).start()
    for k in range(1, near):
        hand_on(0, k, g).start()
    for k in range(1, near):
        xc(k).start()
    xr[g] = xs[g]

    lane_bits = lax.broadcasted_iota(jnp.int32, (8, LANES), 0)
    high_bits = lax.broadcasted_iota(jnp.int32, (groups, LANES), 0)

    def tables(b):
        for k in range(1, near):
            hand_on(b, k, near_id(near - k)).wait_recv()
        for slot in range(*batches[b]):
            both = zh * 0
            t = far_id(slots[slot])
            for bit in range(far.bit_length() - 1):
                both = both + lax.rem(zh // (1 << bit), 2) * lax.rem(t // (1 << bit), 2)
            far_sign = (1 - 2 * lax.rem(both, 2)).astype(jnp.float32)

            @pl.loop(0, near)
            def _(i):
                place = samples[i, slot]
                wide = [parity_sign(lane_bits & place)]
                for bit in range(3, 7):
                    factor = (1 - 2 * ((place >> bit) & 1)).astype(jnp.float32)
                    wide = wide + [w * factor for w in wide]
                had[slot, i] = jnp.concatenate(wide, axis=0).astype(jnp.bfloat16)
                mask[slot, i] = parity_sign(high_bits & (place >> 7)) * far_sign

    tables(0)
    for b in (1, 2):
        first, end = batches[b]
        for slot in range(first, end):
            sc_wait(slots[slot])
        for k in range(1, near):
            if end > first:
                hand_on(b, k, g).start()
    if batches[1][1] > batches[1][0]:
        tables(1)

    for k in range(1, near):
        src = near_id(near - k)
        copy(xs.at[g], xr.at[src], x_send.at[k], x_recv.at[k], near_at(k)).wait_recv()
    for jh in range(groups):
        part = slice(jh * block, (jh + 1) * block)
        for i, value in enumerate(butterfly([xr[d, part] for d in range(near)])):
            hi, lo = split_hi_lo(value)
            mixed[i, part, :LANES] = hi
            mixed[i, part, LANES:] = lo
    def pc(k):
        return copy(part_out.at[k], part_in.at[k], p_send.at[k], p_recv.at[k], far_at(k))

    def partial_sums(order):
        for pair in zip(order[::2], order[1::2]):
            @pl.loop(0, near)
            def _(i):
                table = jnp.concatenate([had[slots.index(k), i] for k in pair], axis=1)
                table = jnp.concatenate([table, table], axis=0)
                product = jnp.dot(mixed[i], table, preferred_element_type=jnp.float32)
                for n, k in enumerate(pair):
                    signs_k = mask[slots.index(k), i]
                    total = None
                    for jh in range(groups):
                        term = product[jh * block : (jh + 1) * block, n * LANES : (n + 1) * LANES] * signs_k[jh : jh + 1]
                        total = term if jh == 0 else total + term
                    part_out[k, i] = total

            for k in pair:
                if k:
                    pc(k).start()

    partial_sums(slots[1:close][::-1])
    tables(2)
    partial_sums(slots[close:][::-1] + [0])
    total = part_out[0]
    for k in slots[1:]:
        pc(k).wait_recv()
        total = total + part_in[k]
    own[g] = total * (1.0 / jnp.sqrt(jnp.float32(length * nx * nz)))
    def own_copy(k):
        return copy(own.at[g], own.at[g], own_send.at[k], own_recv.at[k], near_at(k))

    def row_copy(k):
        return copy(own.at[g], rows.at[col], row_send.at[k], row_recv.at[k], col_at(k))

    for k in range(1, max(cols, near)):
        if k < cols:
            row_copy(k).start()
        if k < near:
            own_copy(k).start()
    rows[col] = own[g]
    for k in range(1, cols):
        src = col_id(cols - k)
        copy(own.at[g], rows.at[src], row_send.at[k], row_recv.at[k], col_at(k)).wait_recv()
    for k in range(1, near):
        src = near_id(near - k)
        copy(own.at[g], own.at[src], own_send.at[k], own_recv.at[k], near_at(k)).wait_recv()
    total = None
    blank = jnp.zeros((width, LANES), jnp.float32)
    odd = lax.rem(col, 2)
    for b in range(near):
        left = jnp.concatenate([rows[turns * d + m, b] for m in range(turns) for d in range(nx)], axis=0)
        right = jnp.concatenate([own[d, b] for d in range(near)], axis=0)
        first = jnp.where(odd == 0, right, blank)
        right = jnp.concatenate([first, right - first], axis=0)
        left_hi, left_lo = split_hi_lo(left)
        right_hi, right_lo = split_hi_lo(right)
        term = lax.dot_general(
            jnp.concatenate([left_hi, left_hi, left_lo], axis=1),
            jnp.concatenate([right_hi, right_lo, right_hi], axis=1),
            (((1,), (1,)), ((), ())),
            preferred_element_type=jnp.float32,
        )
        total = term if b == 0 else total + term
    tile[...] = total.reshape(tile.shape)

    def tc(m):
        target = nx * m + x
        return copy(
            tile.at[m], tile_in.at[zh], t_send.at[m], t_recv.at[zh], {"row": x * nz + 2 * target + zl, "col": col}
        )

    for m in range(turns):
        @pl.when(zh != nx * m + x)
        def _():
            tc(m).start()
    def fc(kx, kc):
        dest = lax.rem(x + kx, nx)
        return copy(
            final.at[dest], gathered.at[col], f_send.at[kx, kc], f_recv.at[col], {"row": dest * nz + z, "col": col_id(kc)}
        )

    @pl.when(x == hub)
    def _():
        total = tile[zh // nx]
        for k in range(1, far):
            src = far_id(far - k)
            copy(tile.at[0], tile_in.at[src], t_send.at[0], t_recv.at[src], far_at(k)).wait_recv()
            total = total + tile_in[src]
        final[...] = total * (1.0 / (LANES * nx * nz))
        gathered[col] = final[x]
        for kx in range(nx):
            for kc in range(cols):
                if kx or kc:
                    fc(kx, kc).start()
    def incoming(k):
        src = col_id(k)
        return copy(final.at[0], gathered.at[src], f_send.at[0, k], f_recv.at[src], col_at(k))

    for k in range(1, cols):
        incoming(k).wait_recv()

    @pl.when(x != hub)
    def _():
        copy(final.at[0], gathered.at[col], f_send.at[0, 1], f_recv.at[col], col_at(1)).wait_recv()

    for b in range(cols // 2):
        gram_ref[:, b * LANES : (b + 1) * LANES] = gathered[2 * b] + gathered[2 * b + 1]

    for d in range(near):
        sketch_ref[d * block : (d + 1) * block, :] = own[d, g]

    for k in range(1, near):
        for b, (first, end) in enumerate(batches):
            if end > first:
                hand_on(b, k, g).wait_send()
        xc(k).wait_send()
        own_copy(k).wait_send()
    for k in range(1, far):
        sc(k).wait_send()
        pc(k).wait_send()
    for k in range(1, cols):
        row_copy(k).wait_send()
    for m in range(turns):
        @pl.when(zh != nx * m + x)
        def _():
            tc(m).wait_send()

    @pl.when(x == hub)
    def _():
        for kx in range(nx):
            for kc in range(cols):
                if kx or kc:
                    fc(kx, kc).wait_send()


def per_device(dims, panel, signs, sample_rows):
    nx, nz, ny, nc = dims
    near, far, cols = 2 * nx, nz // 2, ny * nc
    turns = nz // near
    width, length = panel.shape
    block, groups = width // near, length // LANES
    f32, bf16, i32 = jnp.float32, jnp.bfloat16, jnp.int32
    vmem, dma = pltpu.VMEM, pltpu.SemaphoreType.DMA
    return pl.pallas_call(
        functools.partial(kernel, dims),
        out_shape=(
            jax.ShapeDtypeStruct((width, LANES), f32),
            jax.ShapeDtypeStruct((block, width * cols), f32),
        ),
        in_specs=[pl.BlockSpec(memory_space=pl.ANY)] * 3,
        out_specs=(pl.BlockSpec(memory_space=vmem), pl.BlockSpec(memory_space=vmem)),
        scratch_shapes=[
            vmem((width, length), f32),
            vmem((groups, LANES), i32),
            vmem((1, LANES), i32),
            vmem((near, groups * block, LANES), f32),
            vmem((near, groups * block, LANES), f32),
            vmem((near, far, 1, LANES), i32),
            vmem((far, near, LANES, LANES), bf16),
            vmem((far, near, groups, LANES), f32),
            vmem((near, groups * block, 2 * LANES), bf16),
            vmem((far, near, block, LANES), f32),
            vmem((far, near, block, LANES), f32),
            vmem((near, near, block, LANES), f32),
            vmem((cols, near, block, LANES), f32),
            vmem((turns, nx, block, LANES), f32),
            vmem((far, nx, block, LANES), f32),
            vmem((nx, block, LANES), f32),
            vmem((cols, block, LANES), f32),
            dma((3,)), dma((far,)), dma((far,)), dma((3, near)), dma((3, near)), dma((near,)), dma((near,)),
            dma((far,)), dma((far,)), dma((near,)), dma((near,)), dma((cols,)), dma((cols,)),
            dma((turns,)), dma((far,)), dma((nx, cols)), dma((cols,)),
        ],
        compiler_params=pltpu.CompilerParams(
            collective_id=0, has_side_effects=True, vmem_limit_bytes=60 * 1024 * 1024
        ),
        cost_estimate=pl.CostEstimate(flops=1 << 30, bytes_accessed=1 << 20, transcendentals=0),
    )(panel, signs.reshape(groups, LANES), sample_rows.reshape(1, LANES))


def build(mesh, dims):
    return jax.shard_map(
        functools.partial(per_device, dims),
        mesh=mesh,
        in_specs=(P("col", "row"), P("row"), P("row")),
        out_specs=(P("col", "row"), P("row", None)),
        check_vma=False,
    )


def solution(mesh):
    return build(mesh, (4, 16, 4, 2))
```

```python
import functools

import jax
import jax.numpy as jnp
from jax import lax
from jax.experimental import pallas as pl
from jax.experimental.pallas import tpu as pltpu
from jax.sharding import PartitionSpec as P

MESH = pl.DeviceIdType.MESH
LANES = 128


def parity_sign(bits):
    bits = bits ^ (bits >> 4)
    bits = bits ^ (bits >> 2)
    bits = bits ^ (bits >> 1)
    return (1 - 2 * (bits & 1)).astype(jnp.float32)


def split_hi_lo(value):
    hi = value.astype(jnp.bfloat16)
    return hi, (value - hi.astype(jnp.float32)).astype(jnp.bfloat16)


def butterfly(blocks):
    blocks = list(blocks)
    step = 1
    while step < len(blocks):
        for first in range(len(blocks)):
            if not first & step:
                low, high = blocks[first], blocks[first + step]
                blocks[first], blocks[first + step] = low + high, low - high
        step *= 2
    return blocks


def kernel(
    dims, panel_ref, signs_ref, samp_ref, sketch_ref, gram_ref,
    panel, signs, samp, xs, xr, samples, had, mask, mixed, part_out, part_in,
    own, rows, tile, tile_in, gathered, sketch, gram,
    load_sem, s_send, s_recv, pass_send, pass_recv, x_send, x_recv, p_send, p_recv,
    own_send, own_recv, row_send, row_recv, t_send, t_recv, f_send, f_recv, out_sem,
):
    nx, nz, ny, nc = dims
    width, length = panel.shape
    near, far, cols = 2 * nx, nz // 2, ny * nc
    turns = nz // near
    block = width // near
    groups = length // LANES
    row, col = lax.axis_index("row"), lax.axis_index("col")
    x, z = row // nz, lax.rem(row, nz)
    zh, zl = z // 2, lax.rem(z, 2)
    g = 2 * x + zl

    def copy(src, dst, send, recv, where):
        return pltpu.make_async_remote_copy(
            src_ref=src, dst_ref=dst, send_sem=send, recv_sem=recv,
            device_id=where, device_id_type=MESH,
        )

    def near_id(k):
        return lax.rem(g + k, near)

    def near_at(k):
        other = near_id(k)
        return {"row": (other // 2) * nz + 2 * zh + lax.rem(other, 2), "col": col}

    def far_id(k):
        return lax.rem(zh + k, far)

    def far_at(k):
        return {"row": x * nz + 2 * far_id(k) + zl, "col": col}

    def col_id(k):
        return lax.rem(col + k, cols)

    def col_at(k):
        return {"row": row, "col": col_id(k)}

    hub = lax.rem(zh, nx)

    slots = sorted(range(far), key=lambda k: (min(k, far - k), k))
    close = 1 + sum(0 < min(k, far - k) <= far // 4 for k in slots)
    batches = [(0, 1), (1, close), (close, far)]

    loads = [
        pltpu.make_async_copy(src, dst, load_sem.at[i])
        for i, (src, dst) in enumerate([(samp_ref, samp), (signs_ref, signs), (panel_ref, panel)])
    ]
    for c in loads:
        c.start()

    barrier = pltpu.get_barrier_semaphore()

    def greet(where):
        pl.semaphore_signal(barrier, inc=1, device_id=where, device_id_type=MESH)

    for k in reversed(slots[1:]):
        greet(far_at(k))
    for k in range(1, near):
        greet(near_at(k))
    for k in range(1, cols):
        greet(col_at(k))

    for c in loads:
        c.wait()
    samples[g, 0] = samp[...]
    for jh in range(groups):
        sign = signs[jh : jh + 1, :].astype(jnp.float32)
        signed = panel[:, jh * LANES : (jh + 1) * LANES] * sign
        for d in range(near):
            xs[d, jh * block : (jh + 1) * block, :] = signed[d * block : (d + 1) * block]
    pl.semaphore_wait(barrier, near - 1 + far - 1 + cols - 1)
    def sc(k):
        return copy(samp, samples.at[g, slots.index((far - k) % far)], s_send.at[k], s_recv.at[k], far_at(k))

    def sc_wait(k):
        copy(samp, samples.at[g, slots.index(k)], s_send.at[k], s_recv.at[far - k], far_at(k)).wait_recv()

    def hand_on(b, k, whose):
        first, end = batches[b]
        span = samples.at[whose, pl.ds(first, end - first)]
        return copy(span, span, pass_send.at[b, k], pass_recv.at[b, k], near_at(k))

    def xc(k):
        return copy(xs.at[near_id(k)], xr.at[g], x_send.at[k], x_recv.at[k], near_at(k))

    for k in reversed(slots[1:]):
        sc(k).start()
    for k in range(1, near):
        hand_on(0, k, g).start()
    for k in range(1, near):
        xc(k).start()
    xr[g] = xs[g]

    lane_bits = lax.broadcasted_iota(jnp.int32, (8, LANES), 0)
    high_bits = lax.broadcasted_iota(jnp.int32, (groups, LANES), 0)

    def tables(b):
        for k in range(1, near):
            hand_on(b, k, near_id(near - k)).wait_recv()
        for slot in range(*batches[b]):
            both = zh * 0
            t = far_id(slots[slot])
            for bit in range(far.bit_length() - 1):
                both = both + lax.rem(zh // (1 << bit), 2) * lax.rem(t // (1 << bit), 2)
            far_sign = (1 - 2 * lax.rem(both, 2)).astype(jnp.float32)

            @pl.loop(0, near, unroll=True)
            def _(i):
                place = samples[i, slot]
                wide = [parity_sign(lane_bits & place)]
                for bit in range(3, 7):
                    factor = (1 - 2 * ((place >> bit) & 1)).astype(jnp.float32)
                    wide = wide + [w * factor for w in wide]
                had[slot, i] = jnp.concatenate(wide, axis=0).astype(jnp.bfloat16)
                mask[slot, i] = parity_sign(high_bits & (place >> 7)) * far_sign

    tables(0)
    for b in (1, 2):
        first, end = batches[b]
        for slot in range(first, end):
            sc_wait(slots[slot])
        for k in range(1, near):
            if end > first:
                hand_on(b, k, g).start()
    if batches[1][1] > batches[1][0]:
        tables(1)

    for k in range(1, near):
        src = near_id(near - k)
        copy(xs.at[g], xr.at[src], x_send.at[k], x_recv.at[k], near_at(k)).wait_recv()
    for jh in range(groups):
        part = slice(jh * block, (jh + 1) * block)
        for i, value in enumerate(butterfly([xr[d, part] for d in range(near)])):
            hi, lo = split_hi_lo(value)
            mixed[i, part, :LANES] = hi
            mixed[i, part, LANES:] = lo
    def pc(k):
        return copy(part_out.at[k], part_in.at[k], p_send.at[k], p_recv.at[k], far_at(k))

    def partial_sums(order):
        for pair in zip(order[::2], order[1::2]):
            @pl.loop(0, near, unroll=True)
            def _(i):
                table = jnp.concatenate([had[slots.index(k), i] for k in pair], axis=1)
                table = jnp.concatenate([table, table], axis=0)
                product = jnp.dot(mixed[i], table, preferred_element_type=jnp.float32)
                for n, k in enumerate(pair):
                    signs_k = mask[slots.index(k), i]
                    total = None
                    for jh in range(groups):
                        term = product[jh * block : (jh + 1) * block, n * LANES : (n + 1) * LANES] * signs_k[jh : jh + 1]
                        total = term if jh == 0 else total + term
                    part_out[k, i] = total

            for k in pair:
                if k:
                    pc(k).start()

    partial_sums(slots[1:close][::-1])
    tables(2)
    partial_sums(slots[close:][::-1] + [0])
    total = part_out[0]
    for k in slots[1:]:
        pc(k).wait_recv()
        total = total + part_in[k]
    own[g] = total * (1.0 / jnp.sqrt(jnp.float32(length * nx * nz)))
    def own_copy(k):
        return copy(own.at[g], own.at[g], own_send.at[k], own_recv.at[k], near_at(k))

    def row_copy(k):
        return copy(own.at[g], rows.at[col], row_send.at[k], row_recv.at[k], col_at(k))

    for k in range(1, max(cols, near)):
        if k < cols:
            row_copy(k).start()
        if k < near:
            own_copy(k).start()
    rows[col] = own[g]
    for k in range(1, cols):
        src = col_id(cols - k)
        copy(own.at[g], rows.at[src], row_send.at[k], row_recv.at[k], col_at(k)).wait_recv()
    for k in range(1, near):
        src = near_id(near - k)
        copy(own.at[g], own.at[src], own_send.at[k], own_recv.at[k], near_at(k)).wait_recv()
    total = None
    blank = jnp.zeros((width, LANES), jnp.float32)
    odd = lax.rem(col, 2)
    for b in range(near):
        left = jnp.concatenate([rows[turns * d + m, b] for m in range(turns) for d in range(nx)], axis=0)
        right = jnp.concatenate([own[d, b] for d in range(near)], axis=0)
        first = jnp.where(odd == 0, right, blank)
        right = jnp.concatenate([first, right - first], axis=0)
        left_hi, left_lo = split_hi_lo(left)
        right_hi, right_lo = split_hi_lo(right)
        term = lax.dot_general(
            jnp.concatenate([left_hi, left_hi, left_lo], axis=1),
            jnp.concatenate([right_hi, right_lo, right_hi], axis=1),
            (((1,), (1,)), ((), ())),
            preferred_element_type=jnp.float32,
        )
        total = term if b == 0 else total + term
    tile[...] = total.reshape(tile.shape)

    def mine(m, d):
        return jnp.logical_and(zh == nx * m + x, x == d)

    def tc(m, d):
        where = {"row": d * nz + 2 * (nx * m + x) + zl, "col": col}
        return copy(tile.at[m, d], tile_in.at[zh], t_send.at[m, d], t_recv.at[zh], where)

    def each_tile(act):
        for m in range(turns):
            for d in range(nx):
                @pl.when(jnp.logical_not(mine(m, d)))
                def _():
                    act(tc(m, d))

    each_tile(lambda c: c.start())

    @pl.when(x == hub)
    def _():
        tile_in[zh] = tile[zh // nx, x]

    for d in range(near):
        sketch[d * block : (d + 1) * block, :] = own[d, g]
    outs = [pltpu.make_async_copy(sketch, sketch_ref, out_sem.at[0]), pltpu.make_async_copy(gram, gram_ref, out_sem.at[1])]
    outs[0].start()

    def tile_wait(k):
        src = far_id(k)
        copy(tile.at[0, 0], tile_in.at[src], t_send.at[0, 0], t_recv.at[src], far_at(1)).wait_recv()

    @pl.when(x != hub)
    def _():
        tile_wait(0)

    total = tile_in[zh]
    for k in slots[1:]:
        tile_wait(k)
        total = total + tile_in[far_id(k)]
    gathered[col] = total * (1.0 / (LANES * nx * nz))

    def fc(k):
        return copy(gathered.at[col], gathered.at[col], f_send.at[k], f_recv.at[k], col_at(k))

    for k in range(1, cols):
        fc(k).start()
    for k in range(1, cols):
        there = gathered.at[col_id(cols - k)]
        copy(there, there, f_send.at[k], f_recv.at[k], col_at(k)).wait_recv()
    for b in range(cols // 2):
        gram[:, b * LANES : (b + 1) * LANES] = gathered[2 * b] + gathered[2 * b + 1]
    outs[1].start()

    for k in range(1, near):
        for b, (first, end) in enumerate(batches):
            if end > first:
                hand_on(b, k, g).wait_send()
        xc(k).wait_send()
        own_copy(k).wait_send()
    for k in range(1, far):
        sc(k).wait_send()
        pc(k).wait_send()
    for k in range(1, cols):
        row_copy(k).wait_send()
        fc(k).wait_send()
    each_tile(lambda c: c.wait_send())
    for c in outs:
        c.wait()


def per_device(dims, panel, signs, sample_rows):
    nx, nz, ny, nc = dims
    near, far, cols = 2 * nx, nz // 2, ny * nc
    turns = nz // near
    width, length = panel.shape
    block, groups = width // near, length // LANES
    f32, bf16, i32 = jnp.float32, jnp.bfloat16, jnp.int32
    vmem, dma = pltpu.VMEM, pltpu.SemaphoreType.DMA
    return pl.pallas_call(
        functools.partial(kernel, dims),
        out_shape=(
            jax.ShapeDtypeStruct((width, LANES), f32),
            jax.ShapeDtypeStruct((block, width * cols), f32),
        ),
        in_specs=[pl.BlockSpec(memory_space=pl.ANY)] * 3,
        out_specs=(pl.BlockSpec(memory_space=pl.ANY), pl.BlockSpec(memory_space=pl.ANY)),
        scratch_shapes=[
            vmem((width, length), f32),
            vmem((groups, LANES), i32),
            vmem((1, LANES), i32),
            vmem((near, groups * block, LANES), f32),
            vmem((near, groups * block, LANES), f32),
            vmem((near, far, 1, LANES), i32),
            vmem((far, near, LANES, LANES), bf16),
            vmem((far, near, groups, LANES), f32),
            vmem((near, groups * block, 2 * LANES), bf16),
            vmem((far, near, block, LANES), f32),
            vmem((far, near, block, LANES), f32),
            vmem((near, near, block, LANES), f32),
            vmem((cols, near, block, LANES), f32),
            vmem((turns, nx, block, LANES), f32),
            vmem((far, block, LANES), f32),
            vmem((cols, block, LANES), f32),
            vmem((width, LANES), f32),
            vmem((block, width * cols), f32),
            dma((3,)), dma((far,)), dma((far,)), dma((3, near)), dma((3, near)), dma((near,)), dma((near,)),
            dma((far,)), dma((far,)), dma((near,)), dma((near,)), dma((cols,)), dma((cols,)),
            dma((turns, nx)), dma((far,)), dma((cols,)), dma((cols,)), dma((2,)),
        ],
        compiler_params=pltpu.CompilerParams(
            collective_id=0, has_side_effects=True, vmem_limit_bytes=60 * 1024 * 1024
        ),
        cost_estimate=pl.CostEstimate(flops=1 << 30, bytes_accessed=1 << 20, transcendentals=0),
    )(panel, signs.reshape(groups, LANES), sample_rows.reshape(1, LANES))


def build(mesh, dims):
    return jax.shard_map(
        functools.partial(per_device, dims),
        mesh=mesh,
        in_specs=(P("col", "row"), P("row"), P("row")),
        out_specs=(P("col", "row"), P("row", None)),
        check_vma=False,
    )


def solution(mesh):
    return build(mesh, (4, 16, 4, 2))
```

```python
import functools

import jax
import jax.numpy as jnp
from jax import lax
from jax.experimental import pallas as pl
from jax.experimental.pallas import tpu as pltpu
from jax.sharding import PartitionSpec as P

MESH = pl.DeviceIdType.MESH
LANES = 128


def parity_sign(bits):
    bits = bits ^ (bits >> 4)
    bits = bits ^ (bits >> 2)
    bits = bits ^ (bits >> 1)
    return (1 - 2 * (bits & 1)).astype(jnp.float32)


def split_hi_lo(value):
    hi = value.astype(jnp.bfloat16)
    return hi, (value - hi.astype(jnp.float32)).astype(jnp.bfloat16)


def butterfly(blocks):
    blocks = list(blocks)
    step = 1
    while step < len(blocks):
        for first in range(len(blocks)):
            if not first & step:
                low, high = blocks[first], blocks[first + step]
                blocks[first], blocks[first + step] = low + high, low - high
        step *= 2
    return blocks


def kernel(
    dims, panel_ref, signs_ref, samp_ref, sketch_ref, gram_ref,
    panel, signs, samp, xs, xr, samples, had, mask, mixed, part_out, part_in,
    own, rows, tile, tile_in, gathered, sketch, gram,
    load_sem, s_send, s_recv, pass_send, pass_recv, x_send, x_recv, p_send, p_recv,
    own_send, own_recv, row_send, row_recv, t_send, t_recv, f_send, f_recv, out_sem,
):
    nx, nz, ny, nc = dims
    width, length = panel.shape
    near, far, cols = 2 * nx, nz // 2, ny * nc
    turns = nz // near
    block = width // near
    groups = length // LANES
    row, col = lax.axis_index("row"), lax.axis_index("col")
    x, z = row // nz, lax.rem(row, nz)
    zh, zl = z // 2, lax.rem(z, 2)
    g = 2 * x + zl

    def copy(src, dst, send, recv, where):
        return pltpu.make_async_remote_copy(
            src_ref=src, dst_ref=dst, send_sem=send, recv_sem=recv,
            device_id=where, device_id_type=MESH,
        )

    def near_id(k):
        return lax.rem(g + k, near)

    def near_at(k):
        other = near_id(k)
        return {"row": (other // 2) * nz + 2 * zh + lax.rem(other, 2), "col": col}

    def far_id(k):
        return lax.rem(zh + k, far)

    def far_at(k):
        return {"row": x * nz + 2 * far_id(k) + zl, "col": col}

    def col_id(k):
        return lax.rem(col + k, cols)

    def col_at(k):
        return {"row": row, "col": col_id(k)}

    hub = lax.rem(zh, nx)

    slots = sorted(range(far), key=lambda k: (min(k, far - k), k))
    batches = [(0, 1), (1, far)]

    loads = [
        pltpu.make_async_copy(src, dst, load_sem.at[i])
        for i, (src, dst) in enumerate([(samp_ref, samp), (signs_ref, signs), (panel_ref, panel)])
    ]
    for c in loads:
        c.start()

    barrier = pltpu.get_barrier_semaphore()

    def greet(where):
        pl.semaphore_signal(barrier, inc=1, device_id=where, device_id_type=MESH)

    for k in reversed(slots[1:]):
        greet(far_at(k))
    for k in range(1, near):
        greet(near_at(k))
    for k in range(1, cols):
        greet(col_at(k))

    for c in loads:
        c.wait()
    samples[g, 0] = samp[...]
    for jh in range(groups):
        sign = signs[jh : jh + 1, :].astype(jnp.float32)
        signed = panel[:, jh * LANES : (jh + 1) * LANES] * sign
        for d in range(near):
            xs[d, jh * block : (jh + 1) * block, :] = signed[d * block : (d + 1) * block]
    pl.semaphore_wait(barrier, near - 1 + far - 1 + cols - 1)
    def sc(k):
        return copy(samp, samples.at[g, slots.index((far - k) % far)], s_send.at[k], s_recv.at[k], far_at(k))

    def sc_wait(k):
        copy(samp, samples.at[g, slots.index(k)], s_send.at[k], s_recv.at[far - k], far_at(k)).wait_recv()

    def hand_on(b, k, whose):
        first, end = batches[b]
        span = samples.at[whose, pl.ds(first, end - first)]
        return copy(span, span, pass_send.at[b, k], pass_recv.at[b, k], near_at(k))

    def xc(k):
        return copy(xs.at[near_id(k)], xr.at[g], x_send.at[k], x_recv.at[k], near_at(k))

    for k in reversed(slots[1:]):
        sc(k).start()
    for k in range(1, near):
        hand_on(0, k, g).start()
    for k in range(1, near):
        xc(k).start()
    xr[g] = xs[g]

    lane_bits = lax.broadcasted_iota(jnp.int32, (8, LANES), 0)
    high_bits = lax.broadcasted_iota(jnp.int32, (groups, LANES), 0)

    def tables(b):
        for k in range(1, near):
            hand_on(b, k, near_id(near - k)).wait_recv()
        for slot in range(*batches[b]):
            both = zh * 0
            t = far_id(slots[slot])
            for bit in range(far.bit_length() - 1):
                both = both + lax.rem(zh // (1 << bit), 2) * lax.rem(t // (1 << bit), 2)
            far_sign = (1 - 2 * lax.rem(both, 2)).astype(jnp.float32)

            @pl.loop(0, near, unroll=True)
            def _(i):
                place = samples[i, slot]
                wide = [parity_sign(lane_bits & place)]
                for bit in range(3, 7):
                    factor = (1 - 2 * ((place >> bit) & 1)).astype(jnp.float32)
                    wide = wide + [w * factor for w in wide]
                had[slot, i] = jnp.concatenate(wide, axis=0).astype(jnp.bfloat16)
                mask[slot, i] = parity_sign(high_bits & (place >> 7)) * far_sign

    tables(0)
    for k in slots[1:]:
        sc_wait(k)
    for k in range(1, near):
        hand_on(1, k, g).start()

    for k in range(1, near):
        src = near_id(near - k)
        copy(xs.at[g], xr.at[src], x_send.at[k], x_recv.at[k], near_at(k)).wait_recv()
    for jh in range(groups):
        part = slice(jh * block, (jh + 1) * block)
        for i, value in enumerate(butterfly([xr[d, part] for d in range(near)])):
            hi, lo = split_hi_lo(value)
            mixed[i, part, :LANES] = hi
            mixed[i, part, LANES:] = lo
    def pc(k):
        return copy(part_out.at[k], part_in.at[k], p_send.at[k], p_recv.at[k], far_at(k))

    def partial_sums(order):
        for pair in zip(order[::2], order[1::2]):
            @pl.loop(0, near, unroll=True)
            def _(i):
                table = jnp.concatenate([had[slots.index(k), i] for k in pair], axis=1)
                table = jnp.concatenate([table, table], axis=0)
                product = jnp.dot(mixed[i], table, preferred_element_type=jnp.float32)
                for n, k in enumerate(pair):
                    signs_k = mask[slots.index(k), i]
                    total = None
                    for jh in range(groups):
                        term = product[jh * block : (jh + 1) * block, n * LANES : (n + 1) * LANES] * signs_k[jh : jh + 1]
                        total = term if jh == 0 else total + term
                    part_out[k, i] = total

            for k in pair:
                if k:
                    pc(k).start()

    tables(1)
    partial_sums(slots[::-1])
    total = part_out[0]
    for k in slots[1:]:
        pc(k).wait_recv()
        total = total + part_in[k]
    own[g] = total * (1.0 / jnp.sqrt(jnp.float32(length * nx * nz)))
    def own_copy(k):
        return copy(own.at[g], own.at[g], own_send.at[k], own_recv.at[k], near_at(k))

    def row_copy(k):
        return copy(own.at[g], rows.at[col], row_send.at[k], row_recv.at[k], col_at(k))

    for k in range(1, max(cols, near)):
        if k < cols:
            row_copy(k).start()
        if k < near:
            own_copy(k).start()
    rows[col] = own[g]
    for k in range(1, cols):
        src = col_id(cols - k)
        copy(own.at[g], rows.at[src], row_send.at[k], row_recv.at[k], col_at(k)).wait_recv()
    for k in range(1, near):
        src = near_id(near - k)
        copy(own.at[g], own.at[src], own_send.at[k], own_recv.at[k], near_at(k)).wait_recv()
    total = None
    blank = jnp.zeros((width, LANES), jnp.float32)
    odd = lax.rem(col, 2)
    for b in range(near):
        left = jnp.concatenate([rows[turns * d + m, b] for m in range(turns) for d in range(nx)], axis=0)
        right = jnp.concatenate([own[d, b] for d in range(near)], axis=0)
        first = jnp.where(odd == 0, right, blank)
        right = jnp.concatenate([first, right - first], axis=0)
        left_hi, left_lo = split_hi_lo(left)
        right_hi, right_lo = split_hi_lo(right)
        term = lax.dot_general(
            jnp.concatenate([left_hi, left_hi, left_lo], axis=1),
            jnp.concatenate([right_hi, right_lo, right_hi], axis=1),
            (((1,), (1,)), ((), ())),
            preferred_element_type=jnp.float32,
        )
        total = term if b == 0 else total + term
    tile[...] = total.reshape(tile.shape)

    def mine(m, d):
        return jnp.logical_and(zh == nx * m + x, x == d)

    def tc(m, d):
        where = {"row": d * nz + 2 * (nx * m + x) + zl, "col": col}
        return copy(tile.at[m, d], tile_in.at[zh], t_send.at[m, d], t_recv.at[zh], where)

    def each_tile(act):
        for m in range(turns):
            for d in range(nx):
                @pl.when(jnp.logical_not(mine(m, d)))
                def _():
                    act(tc(m, d))

    each_tile(lambda c: c.start())

    @pl.when(x == hub)
    def _():
        tile_in[zh] = tile[zh // nx, x]

    for d in range(near):
        sketch[d * block : (d + 1) * block, :] = own[d, g]
    outs = [pltpu.make_async_copy(sketch, sketch_ref, out_sem.at[0]), pltpu.make_async_copy(gram, gram_ref, out_sem.at[1])]
    outs[0].start()

    def tile_wait(k):
        src = far_id(k)
        copy(tile.at[0, 0], tile_in.at[src], t_send.at[0, 0], t_recv.at[src], far_at(1)).wait_recv()

    @pl.when(x != hub)
    def _():
        tile_wait(0)

    total = tile_in[zh]
    for k in slots[1:]:
        tile_wait(k)
        total = total + tile_in[far_id(k)]
    gathered[col] = total * (1.0 / (LANES * nx * nz))

    def fc(k):
        return copy(gathered.at[col], gathered.at[col], f_send.at[k], f_recv.at[k], col_at(k))

    for k in range(1, cols):
        fc(k).start()
    for k in range(1, cols):
        there = gathered.at[col_id(cols - k)]
        copy(there, there, f_send.at[k], f_recv.at[k], col_at(k)).wait_recv()
    for b in range(cols // 2):
        gram[:, b * LANES : (b + 1) * LANES] = gathered[2 * b] + gathered[2 * b + 1]
    outs[1].start()

    for k in range(1, near):
        for b in range(2):
            hand_on(b, k, g).wait_send()
        xc(k).wait_send()
        own_copy(k).wait_send()
    for k in range(1, far):
        sc(k).wait_send()
        pc(k).wait_send()
    for k in range(1, cols):
        row_copy(k).wait_send()
        fc(k).wait_send()
    each_tile(lambda c: c.wait_send())
    for c in outs:
        c.wait()


def per_device(dims, panel, signs, sample_rows):
    nx, nz, ny, nc = dims
    near, far, cols = 2 * nx, nz // 2, ny * nc
    turns = nz // near
    width, length = panel.shape
    block, groups = width // near, length // LANES
    f32, bf16, i32 = jnp.float32, jnp.bfloat16, jnp.int32
    vmem, dma = pltpu.VMEM, pltpu.SemaphoreType.DMA
    return pl.pallas_call(
        functools.partial(kernel, dims),
        out_shape=(
            jax.ShapeDtypeStruct((width, LANES), f32),
            jax.ShapeDtypeStruct((block, width * cols), f32),
        ),
        in_specs=[pl.BlockSpec(memory_space=pl.ANY)] * 3,
        out_specs=(pl.BlockSpec(memory_space=pl.ANY), pl.BlockSpec(memory_space=pl.ANY)),
        scratch_shapes=[
            vmem((width, length), f32),
            vmem((groups, LANES), i32),
            vmem((1, LANES), i32),
            vmem((near, groups * block, LANES), f32),
            vmem((near, groups * block, LANES), f32),
            vmem((near, far, 1, LANES), i32),
            vmem((far, near, LANES, LANES), bf16),
            vmem((far, near, groups, LANES), f32),
            vmem((near, groups * block, 2 * LANES), bf16),
            vmem((far, near, block, LANES), f32),
            vmem((far, near, block, LANES), f32),
            vmem((near, near, block, LANES), f32),
            vmem((cols, near, block, LANES), f32),
            vmem((turns, nx, block, LANES), f32),
            vmem((far, block, LANES), f32),
            vmem((cols, block, LANES), f32),
            vmem((width, LANES), f32),
            vmem((block, width * cols), f32),
            dma((3,)), dma((far,)), dma((far,)), dma((2, near)), dma((2, near)), dma((near,)), dma((near,)),
            dma((far,)), dma((far,)), dma((near,)), dma((near,)), dma((cols,)), dma((cols,)),
            dma((turns, nx)), dma((far,)), dma((cols,)), dma((cols,)), dma((2,)),
        ],
        compiler_params=pltpu.CompilerParams(
            collective_id=0, has_side_effects=True, vmem_limit_bytes=60 * 1024 * 1024
        ),
        cost_estimate=pl.CostEstimate(flops=1 << 30, bytes_accessed=1 << 20, transcendentals=0),
    )(panel, signs.reshape(groups, LANES), sample_rows.reshape(1, LANES))


def build(mesh, dims):
    return jax.shard_map(
        functools.partial(per_device, dims),
        mesh=mesh,
        in_specs=(P("col", "row"), P("row"), P("row")),
        out_specs=(P("col", "row"), P("row", None)),
        check_vma=False,
    )


def solution(mesh):
    return build(mesh, (4, 16, 4, 2))
```

```python
import functools

import jax
import jax.numpy as jnp
from jax import lax
from jax.experimental import pallas as pl
from jax.experimental.pallas import tpu as pltpu
from jax.sharding import PartitionSpec as P

MESH = pl.DeviceIdType.MESH
LANES = 128


def parity_sign(bits):
    bits = bits ^ (bits >> 4)
    bits = bits ^ (bits >> 2)
    bits = bits ^ (bits >> 1)
    return (1 - 2 * (bits & 1)).astype(jnp.float32)


def split_hi_lo(value):
    hi = value.astype(jnp.bfloat16)
    return hi, (value - hi.astype(jnp.float32)).astype(jnp.bfloat16)


def butterfly(blocks):
    blocks = list(blocks)
    step = 1
    while step < len(blocks):
        for first in range(len(blocks)):
            if not first & step:
                low, high = blocks[first], blocks[first + step]
                blocks[first], blocks[first + step] = low + high, low - high
        step *= 2
    return blocks


def kernel(
    dims, panel_ref, signs_ref, samp_ref, sketch_ref, gram_ref,
    panel, signs, samp, xs, xr, samples, had, mask, mixed, part_out, part_in,
    own, rows, tile, tile_in, gathered, sketch, gram,
    load_sem, s_send, s_recv, pass_send, pass_recv, x_send, x_recv, p_send, p_recv,
    own_send, own_recv, row_send, row_recv, t_send, t_recv, f_send, f_recv, out_sem,
):
    nx, nz, ny, nc = dims
    width, length = panel.shape
    near, far, cols = 2 * nx, nz // 2, ny * nc
    turns = nz // near
    block = width // near
    groups = length // LANES
    row, col = lax.axis_index("row"), lax.axis_index("col")
    x, z = row // nz, lax.rem(row, nz)
    zh, zl = z // 2, lax.rem(z, 2)
    g = 2 * x + zl

    def copy(src, dst, send, recv, where):
        return pltpu.make_async_remote_copy(
            src_ref=src, dst_ref=dst, send_sem=send, recv_sem=recv,
            device_id=where, device_id_type=MESH,
        )

    def near_id(k):
        return lax.rem(g + k, near)

    def near_at(k):
        other = near_id(k)
        return {"row": (other // 2) * nz + 2 * zh + lax.rem(other, 2), "col": col}

    def far_id(k):
        return lax.rem(zh + k, far)

    def far_at(k):
        return {"row": x * nz + 2 * far_id(k) + zl, "col": col}

    def col_id(k):
        return lax.rem(col + k, cols)

    def col_at(k):
        return {"row": row, "col": col_id(k)}

    hub = lax.rem(zh, nx)

    slots = sorted(range(far), key=lambda k: (min(k, far - k), k))
    batches = [(0, 1), (1, far)]

    loads = [
        pltpu.make_async_copy(src, dst, load_sem.at[i])
        for i, (src, dst) in enumerate([(samp_ref, samp), (signs_ref, signs), (panel_ref, panel)])
    ]
    for c in loads:
        c.start()

    barrier = pltpu.get_barrier_semaphore()

    def greet(where):
        pl.semaphore_signal(barrier, inc=1, device_id=where, device_id_type=MESH)

    for k in reversed(slots[1:]):
        greet(far_at(k))
    for k in range(1, near):
        greet(near_at(k))
    for k in range(1, cols):
        greet(col_at(k))

    for c in loads:
        c.wait()
    samples[g, 0] = samp[...]
    for jh in range(groups):
        sign = signs[jh : jh + 1, :].astype(jnp.float32)
        signed = panel[:, jh * LANES : (jh + 1) * LANES] * sign
        for d in range(near):
            xs[d, jh * block : (jh + 1) * block, :] = signed[d * block : (d + 1) * block]
    pl.semaphore_wait(barrier, near - 1 + far - 1 + cols - 1)
    def sc(k):
        return copy(samp, samples.at[g, slots.index((far - k) % far)], s_send.at[k], s_recv.at[k], far_at(k))

    def sc_wait(k):
        copy(samp, samples.at[g, slots.index(k)], s_send.at[k], s_recv.at[far - k], far_at(k)).wait_recv()

    def hand_on(b, k, whose):
        first, end = batches[b]
        span = samples.at[whose, pl.ds(first, end - first)]
        return copy(span, span, pass_send.at[b, k], pass_recv.at[b, k], near_at(k))

    def xc(k):
        return copy(xs.at[near_id(k)], xr.at[g], x_send.at[k], x_recv.at[k], near_at(k))

    for k in reversed(slots[1:]):
        sc(k).start()
    for k in range(1, near):
        hand_on(0, k, g).start()
    for k in range(1, near):
        xc(k).start()
    xr[g] = xs[g]

    lane_bits = lax.broadcasted_iota(jnp.int32, (8, LANES), 0)
    high_bits = lax.broadcasted_iota(jnp.int32, (groups, LANES), 0)

    def passed_on(b):
        for k in range(1, near):
            hand_on(b, k, near_id(near - k)).wait_recv()

    def tables(slot):
        both = zh * 0
        t = far_id(slots[slot])
        for bit in range(far.bit_length() - 1):
            both = both + lax.rem(zh // (1 << bit), 2) * lax.rem(t // (1 << bit), 2)
        far_sign = (1 - 2 * lax.rem(both, 2)).astype(jnp.float32)

        @pl.loop(0, near, unroll=True)
        def _(i):
            place = samples[i, slot]
            wide = [parity_sign(lane_bits & place)]
            for bit in range(3, 7):
                factor = (1 - 2 * ((place >> bit) & 1)).astype(jnp.float32)
                wide = wide + [w * factor for w in wide]
            had[slot, i] = jnp.concatenate(wide, axis=0).astype(jnp.bfloat16)
            mask[slot, i] = parity_sign(high_bits & (place >> 7)) * far_sign

    passed_on(0)
    tables(0)
    for k in slots[1:]:
        sc_wait(k)
    for k in range(1, near):
        hand_on(1, k, g).start()

    for k in range(1, near):
        src = near_id(near - k)
        copy(xs.at[g], xr.at[src], x_send.at[k], x_recv.at[k], near_at(k)).wait_recv()
    for jh in range(groups):
        part = slice(jh * block, (jh + 1) * block)
        for i, value in enumerate(butterfly([xr[d, part] for d in range(near)])):
            hi, lo = split_hi_lo(value)
            mixed[i, part, :LANES] = hi
            mixed[i, part, LANES:] = lo
    def pc(k):
        return copy(part_out.at[k], part_in.at[k], p_send.at[k], p_recv.at[k], far_at(k))

    def partial_sums(order):
        for pair in zip(order[::2], order[1::2]):
            for k in pair:
                if k:
                    tables(slots.index(k))

            @pl.loop(0, near, unroll=True)
            def _(i):
                table = jnp.concatenate([had[slots.index(k), i] for k in pair], axis=1)
                table = jnp.concatenate([table, table], axis=0)
                product = jnp.dot(mixed[i], table, preferred_element_type=jnp.float32)
                for n, k in enumerate(pair):
                    signs_k = mask[slots.index(k), i]
                    total = None
                    for jh in range(groups):
                        term = product[jh * block : (jh + 1) * block, n * LANES : (n + 1) * LANES] * signs_k[jh : jh + 1]
                        total = term if jh == 0 else total + term
                    part_out[k, i] = total

            for k in pair:
                if k:
                    pc(k).start()

    passed_on(1)
    partial_sums(slots[::-1])
    total = part_out[0]
    for k in slots[1:]:
        pc(k).wait_recv()
        total = total + part_in[k]
    own[g] = total * (1.0 / jnp.sqrt(jnp.float32(length * nx * nz)))
    def own_copy(k):
        return copy(own.at[g], own.at[g], own_send.at[k], own_recv.at[k], near_at(k))

    def row_copy(k):
        return copy(own.at[g], rows.at[col], row_send.at[k], row_recv.at[k], col_at(k))

    for k in range(1, max(cols, near)):
        if k < cols:
            row_copy(k).start()
        if k < near:
            own_copy(k).start()
    rows[col] = own[g]
    for k in range(1, cols):
        src = col_id(cols - k)
        copy(own.at[g], rows.at[src], row_send.at[k], row_recv.at[k], col_at(k)).wait_recv()
    for k in range(1, near):
        src = near_id(near - k)
        copy(own.at[g], own.at[src], own_send.at[k], own_recv.at[k], near_at(k)).wait_recv()
    total = None
    blank = jnp.zeros((width, LANES), jnp.float32)
    odd = lax.rem(col, 2)
    for b in range(near):
        left = jnp.concatenate([rows[turns * d + m, b] for m in range(turns) for d in range(nx)], axis=0)
        right = jnp.concatenate([own[d, b] for d in range(near)], axis=0)
        first = jnp.where(odd == 0, right, blank)
        right = jnp.concatenate([first, right - first], axis=0)
        left_hi, left_lo = split_hi_lo(left)
        right_hi, right_lo = split_hi_lo(right)
        term = lax.dot_general(
            jnp.concatenate([left_hi, left_hi, left_lo], axis=1),
            jnp.concatenate([right_hi, right_lo, right_hi], axis=1),
            (((1,), (1,)), ((), ())),
            preferred_element_type=jnp.float32,
        )
        total = term if b == 0 else total + term
    tile[...] = total.reshape(tile.shape)

    def mine(m, d):
        return jnp.logical_and(zh == nx * m + x, x == d)

    def tc(m, d):
        where = {"row": d * nz + 2 * (nx * m + x) + zl, "col": col}
        return copy(tile.at[m, d], tile_in.at[zh], t_send.at[m, d], t_recv.at[zh], where)

    def each_tile(act):
        for m in range(turns):
            for d in range(nx):
                @pl.when(jnp.logical_not(mine(m, d)))
                def _():
                    act(tc(m, d))

    each_tile(lambda c: c.start())

    @pl.when(x == hub)
    def _():
        tile_in[zh] = tile[zh // nx, x]

    for d in range(near):
        sketch[d * block : (d + 1) * block, :] = own[d, g]
    outs = [pltpu.make_async_copy(sketch, sketch_ref, out_sem.at[0]), pltpu.make_async_copy(gram, gram_ref, out_sem.at[1])]
    outs[0].start()

    def tile_wait(k):
        src = far_id(k)
        copy(tile.at[0, 0], tile_in.at[src], t_send.at[0, 0], t_recv.at[src], far_at(1)).wait_recv()

    @pl.when(x != hub)
    def _():
        tile_wait(0)

    total = tile_in[zh]
    for k in slots[1:]:
        tile_wait(k)
        total = total + tile_in[far_id(k)]
    gathered[col] = total * (1.0 / (LANES * nx * nz))

    def fc(k):
        return copy(gathered.at[col], gathered.at[col], f_send.at[k], f_recv.at[k], col_at(k))

    for k in range(1, cols):
        fc(k).start()
    for k in range(1, cols):
        there = gathered.at[col_id(cols - k)]
        copy(there, there, f_send.at[k], f_recv.at[k], col_at(k)).wait_recv()
    for b in range(cols // 2):
        gram[:, b * LANES : (b + 1) * LANES] = gathered[2 * b] + gathered[2 * b + 1]
    outs[1].start()

    for k in range(1, near):
        for b in range(2):
            hand_on(b, k, g).wait_send()
        xc(k).wait_send()
        own_copy(k).wait_send()
    for k in range(1, far):
        sc(k).wait_send()
        pc(k).wait_send()
    for k in range(1, cols):
        row_copy(k).wait_send()
        fc(k).wait_send()
    each_tile(lambda c: c.wait_send())
    for c in outs:
        c.wait()


def per_device(dims, panel, signs, sample_rows):
    nx, nz, ny, nc = dims
    near, far, cols = 2 * nx, nz // 2, ny * nc
    turns = nz // near
    width, length = panel.shape
    block, groups = width // near, length // LANES
    f32, bf16, i32 = jnp.float32, jnp.bfloat16, jnp.int32
    vmem, dma = pltpu.VMEM, pltpu.SemaphoreType.DMA
    return pl.pallas_call(
        functools.partial(kernel, dims),
        out_shape=(
            jax.ShapeDtypeStruct((width, LANES), f32),
            jax.ShapeDtypeStruct((block, width * cols), f32),
        ),
        in_specs=[pl.BlockSpec(memory_space=pl.ANY)] * 3,
        out_specs=(pl.BlockSpec(memory_space=pl.ANY), pl.BlockSpec(memory_space=pl.ANY)),
        scratch_shapes=[
            vmem((width, length), f32),
            vmem((groups, LANES), i32),
            vmem((1, LANES), i32),
            vmem((near, groups * block, LANES), f32),
            vmem((near, groups * block, LANES), f32),
            vmem((near, far, 1, LANES), i32),
            vmem((far, near, LANES, LANES), bf16),
            vmem((far, near, groups, LANES), f32),
            vmem((near, groups * block, 2 * LANES), bf16),
            vmem((far, near, block, LANES), f32),
            vmem((far, near, block, LANES), f32),
            vmem((near, near, block, LANES), f32),
            vmem((cols, near, block, LANES), f32),
            vmem((turns, nx, block, LANES), f32),
            vmem((far, block, LANES), f32),
            vmem((cols, block, LANES), f32),
            vmem((width, LANES), f32),
            vmem((block, width * cols), f32),
            dma((3,)), dma((far,)), dma((far,)), dma((2, near)), dma((2, near)), dma((near,)), dma((near,)),
            dma((far,)), dma((far,)), dma((near,)), dma((near,)), dma((cols,)), dma((cols,)),
            dma((turns, nx)), dma((far,)), dma((cols,)), dma((cols,)), dma((2,)),
        ],
        compiler_params=pltpu.CompilerParams(
            collective_id=0, has_side_effects=True, vmem_limit_bytes=60 * 1024 * 1024
        ),
        cost_estimate=pl.CostEstimate(flops=1 << 30, bytes_accessed=1 << 20, transcendentals=0),
    )(panel, signs.reshape(groups, LANES), sample_rows.reshape(1, LANES))


def build(mesh, dims):
    return jax.shard_map(
        functools.partial(per_device, dims),
        mesh=mesh,
        in_specs=(P("col", "row"), P("row"), P("row")),
        out_specs=(P("col", "row"), P("row", None)),
        check_vma=False,
    )


def solution(mesh):
    return build(mesh, (4, 16, 4, 2))
```

```python
import functools

import jax
import jax.numpy as jnp
from jax import lax
from jax.experimental import pallas as pl
from jax.experimental.pallas import tpu as pltpu
from jax.sharding import PartitionSpec as P

MESH = pl.DeviceIdType.MESH
LANES = 128


def parity_sign(bits):
    bits = bits ^ (bits >> 4)
    bits = bits ^ (bits >> 2)
    bits = bits ^ (bits >> 1)
    return (1 - 2 * (bits & 1)).astype(jnp.float32)


def split_hi_lo(value):
    hi = value.astype(jnp.bfloat16)
    return hi, (value - hi.astype(jnp.float32)).astype(jnp.bfloat16)


def butterfly(blocks):
    blocks = list(blocks)
    step = 1
    while step < len(blocks):
        for first in range(len(blocks)):
            if not first & step:
                low, high = blocks[first], blocks[first + step]
                blocks[first], blocks[first + step] = low + high, low - high
        step *= 2
    return blocks


def kernel(
    dims, panel_ref, signs_ref, samp_ref, sketch_ref, gram_ref,
    panel, signs, samp, xs, xr, samples, had, mask, mixed, part_out, part_in,
    own, rows, tile, tile_in, gathered, sketch, gram,
    load_sem, s_send, s_recv, pass_send, pass_recv, x_send, x_recv, p_send, p_recv,
    own_send, own_recv, row_send, row_recv, t_send, t_recv, f_send, f_recv, out_sem,
):
    nx, nz, ny, nc = dims
    width, length = panel.shape
    near, far, cols = 2 * nx, nz // 2, ny * nc
    turns = nz // near
    block = width // near
    groups = length // LANES
    row, col = lax.axis_index("row"), lax.axis_index("col")
    x, z = row // nz, lax.rem(row, nz)
    zh, zl = z // 2, lax.rem(z, 2)
    g = 2 * x + zl

    def copy(src, dst, send, recv, where):
        return pltpu.make_async_remote_copy(
            src_ref=src, dst_ref=dst, send_sem=send, recv_sem=recv,
            device_id=where, device_id_type=MESH,
        )

    def near_id(k):
        return lax.rem(g + k, near)

    def near_at(k):
        other = near_id(k)
        return {"row": (other // 2) * nz + 2 * zh + lax.rem(other, 2), "col": col}

    def far_id(k):
        return lax.rem(zh + k, far)

    def far_at(k):
        return {"row": x * nz + 2 * far_id(k) + zl, "col": col}

    def col_id(k):
        return lax.rem(col + k, cols)

    def col_at(k):
        return {"row": row, "col": col_id(k)}

    hub = lax.rem(zh, nx)

    slots = sorted(range(far), key=lambda k: (min(k, far - k), k))
    batches = [(0, 1), (1, far)]

    loads = [
        pltpu.make_async_copy(src, dst, load_sem.at[i])
        for i, (src, dst) in enumerate([(samp_ref, samp), (signs_ref, signs), (panel_ref, panel)])
    ]
    for c in loads:
        c.start()

    barrier = pltpu.get_barrier_semaphore()

    def greet(where):
        pl.semaphore_signal(barrier, inc=1, device_id=where, device_id_type=MESH)

    for k in reversed(slots[1:]):
        greet(far_at(k))
    for k in range(1, near):
        greet(near_at(k))
    for k in range(1, cols):
        greet(col_at(k))

    for c in loads:
        c.wait()
    samples[g, 0] = samp[...]
    for jh in range(groups):
        sign = signs[jh : jh + 1, :].astype(jnp.float32)
        signed = panel[:, jh * LANES : (jh + 1) * LANES] * sign
        for d in range(near):
            xs[d, jh * block : (jh + 1) * block, :] = signed[d * block : (d + 1) * block]
    pl.semaphore_wait(barrier, near - 1 + far - 1 + cols - 1)
    def sc(k):
        return copy(samp, samples.at[g, slots.index((far - k) % far)], s_send.at[k], s_recv.at[k], far_at(k))

    def sc_wait(k):
        copy(samp, samples.at[g, slots.index(k)], s_send.at[k], s_recv.at[far - k], far_at(k)).wait_recv()

    def hand_on(b, k, whose):
        first, end = batches[b]
        span = samples.at[whose, pl.ds(first, end - first)]
        return copy(span, span, pass_send.at[b, k], pass_recv.at[b, k], near_at(k))

    def xc(k):
        return copy(xs.at[near_id(k)], xr.at[g], x_send.at[k], x_recv.at[k], near_at(k))

    for k in reversed(slots[1:]):
        sc(k).start()
    for k in range(1, near):
        hand_on(0, k, g).start()
    for k in range(1, near):
        xc(k).start()
    xr[g] = xs[g]

    lane_bits = lax.broadcasted_iota(jnp.int32, (8, LANES), 0)
    high_bits = lax.broadcasted_iota(jnp.int32, (groups, LANES), 0)

    def passed_on(b):
        for k in range(1, near):
            hand_on(b, k, near_id(near - k)).wait_recv()

    def tables(slot):
        both = zh * 0
        t = far_id(slots[slot])
        for bit in range(far.bit_length() - 1):
            both = both + lax.rem(zh // (1 << bit), 2) * lax.rem(t // (1 << bit), 2)
        far_sign = (1 - 2 * lax.rem(both, 2)).astype(jnp.float32)

        @pl.loop(0, near, unroll=True)
        def _(i):
            place = samples[i, slot]
            wide = [parity_sign(lane_bits & place)]
            for bit in range(3, 7):
                factor = (1 - 2 * ((place >> bit) & 1)).astype(jnp.float32)
                wide = wide + [w * factor for w in wide]
            had[slot, i] = jnp.concatenate(wide, axis=0).astype(jnp.bfloat16)
            mask[slot, i] = parity_sign(high_bits & (place >> 7)) * far_sign

    passed_on(0)
    tables(0)
    for k in slots[1:]:
        sc_wait(k)
    for k in range(1, near):
        hand_on(1, k, g).start()

    for k in range(1, near):
        src = near_id(near - k)
        copy(xs.at[g], xr.at[src], x_send.at[k], x_recv.at[k], near_at(k)).wait_recv()
    for jh in range(groups):
        part = slice(jh * block, (jh + 1) * block)
        for i, value in enumerate(butterfly([xr[d, part] for d in range(near)])):
            hi, lo = split_hi_lo(value)
            mixed[i, part, :LANES] = hi
            mixed[i, part, LANES:] = lo
    def pc(k):
        return copy(part_out.at[k], part_in.at[k], p_send.at[k], p_recv.at[k], far_at(k))

    def partial_sums(order):
        for pair in zip(order[::2], order[1::2]):
            for k in pair:
                if k:
                    tables(slots.index(k))

            @pl.loop(0, near, unroll=True)
            def _(i):
                table = jnp.concatenate([had[slots.index(k), i] for k in pair], axis=1)
                table = jnp.concatenate([table, table], axis=0)
                product = jnp.dot(mixed[i], table, preferred_element_type=jnp.float32)
                for n, k in enumerate(pair):
                    signs_k = mask[slots.index(k), i]
                    total = None
                    for jh in range(groups):
                        term = product[jh * block : (jh + 1) * block, n * LANES : (n + 1) * LANES] * signs_k[jh : jh + 1]
                        total = term if jh == 0 else total + term
                    part_out[k, i] = total

            for k in pair:
                if k:
                    pc(k).start()

    passed_on(1)
    partial_sums(slots[::-1])
    total = part_out[0]
    for k in slots[1:]:
        pc(k).wait_recv()
        total = total + part_in[k]
    own[g] = total * (1.0 / jnp.sqrt(jnp.float32(length * nx * nz)))
    def own_copy(k):
        return copy(own.at[g], own.at[g], own_send.at[k], own_recv.at[k], near_at(k))

    def row_copy(k):
        return copy(own.at[g], rows.at[col], row_send.at[k], row_recv.at[k], col_at(k))

    for k in range(1, max(cols, near)):
        if k < cols:
            row_copy(k).start()
        if k < near:
            own_copy(k).start()
    rows[col] = own[g]
    for k in range(1, cols):
        src = col_id(cols - k)
        copy(own.at[g], rows.at[src], row_send.at[k], row_recv.at[k], col_at(k)).wait_recv()
    for k in range(1, near):
        src = near_id(near - k)
        copy(own.at[g], own.at[src], own_send.at[k], own_recv.at[k], near_at(k)).wait_recv()
    total = None
    blank = jnp.zeros((width, LANES), jnp.float32)
    odd = lax.rem(col, 2)
    for b in range(near):
        left = jnp.concatenate([rows[turns * d + m, b] for m in range(turns) for d in range(nx)], axis=0)
        right = jnp.concatenate([own[d, b] for d in range(near)], axis=0)
        first = jnp.where(odd == 0, right, blank)
        right = jnp.concatenate([first, right - first], axis=0)
        left_hi, left_lo = split_hi_lo(left)
        right_hi, right_lo = split_hi_lo(right)
        term = lax.dot_general(
            jnp.concatenate([left_hi, left_hi, left_lo], axis=1),
            jnp.concatenate([right_hi, right_lo, right_hi], axis=1),
            (((1,), (1,)), ((), ())),
            preferred_element_type=jnp.float32,
        )
        total = term if b == 0 else total + term
    tile[...] = total.reshape(tile.shape)

    def mine(m, d):
        return jnp.logical_and(zh == nx * m + x, x == d)

    def tc(m, d):
        where = {"row": d * nz + 2 * (nx * m + x) + zl, "col": col}
        return copy(tile.at[m, d], tile_in.at[zh], t_send.at[m, d], t_recv.at[zh], where)

    def each_tile(act):
        for m in range(turns):
            for d in range(nx):
                @pl.when(jnp.logical_not(mine(m, d)))
                def _():
                    act(tc(m, d))

    each_tile(lambda c: c.start())

    @pl.when(x == hub)
    def _():
        tile_in[zh] = tile[zh // nx, x]

    for d in range(near):
        sketch[d * block : (d + 1) * block, :] = own[d, g]
    outs = [pltpu.make_async_copy(sketch, sketch_ref, out_sem.at[0]), pltpu.make_async_copy(gram, gram_ref, out_sem.at[1])]
    outs[0].start()

    for k in range(1, near):
        for b in range(2):
            hand_on(b, k, g).wait_send()
        xc(k).wait_send()
        own_copy(k).wait_send()
    for k in range(1, far):
        sc(k).wait_send()
        pc(k).wait_send()
    for k in range(1, cols):
        row_copy(k).wait_send()

    def tile_wait(k):
        src = far_id(k)
        copy(tile.at[0, 0], tile_in.at[src], t_send.at[0, 0], t_recv.at[src], far_at(1)).wait_recv()

    @pl.when(x != hub)
    def _():
        tile_wait(0)

    total = tile_in[zh]
    for k in slots[1:]:
        tile_wait(k)
        total = total + tile_in[far_id(k)]
    gathered[col] = total * (1.0 / (LANES * nx * nz))

    def fc(k):
        return copy(gathered.at[col], gathered.at[col], f_send.at[k], f_recv.at[k], col_at(k))

    for k in range(1, cols):
        fc(k).start()
    for k in range(1, cols):
        there = gathered.at[col_id(cols - k)]
        copy(there, there, f_send.at[k], f_recv.at[k], col_at(k)).wait_recv()
    for b in range(cols // 2):
        gram[:, b * LANES : (b + 1) * LANES] = gathered[2 * b] + gathered[2 * b + 1]
    outs[1].start()

    for k in range(1, cols):
        fc(k).wait_send()
    each_tile(lambda c: c.wait_send())
    for c in outs:
        c.wait()


def per_device(dims, panel, signs, sample_rows):
    nx, nz, ny, nc = dims
    near, far, cols = 2 * nx, nz // 2, ny * nc
    turns = nz // near
    width, length = panel.shape
    block, groups = width // near, length // LANES
    f32, bf16, i32 = jnp.float32, jnp.bfloat16, jnp.int32
    vmem, dma = pltpu.VMEM, pltpu.SemaphoreType.DMA
    return pl.pallas_call(
        functools.partial(kernel, dims),
        out_shape=(
            jax.ShapeDtypeStruct((width, LANES), f32),
            jax.ShapeDtypeStruct((block, width * cols), f32),
        ),
        in_specs=[pl.BlockSpec(memory_space=pl.ANY)] * 3,
        out_specs=(pl.BlockSpec(memory_space=pl.ANY), pl.BlockSpec(memory_space=pl.ANY)),
        scratch_shapes=[
            vmem((width, length), f32),
            vmem((groups, LANES), i32),
            vmem((1, LANES), i32),
            vmem((near, groups * block, LANES), f32),
            vmem((near, groups * block, LANES), f32),
            vmem((near, far, 1, LANES), i32),
            vmem((far, near, LANES, LANES), bf16),
            vmem((far, near, groups, LANES), f32),
            vmem((near, groups * block, 2 * LANES), bf16),
            vmem((far, near, block, LANES), f32),
            vmem((far, near, block, LANES), f32),
            vmem((near, near, block, LANES), f32),
            vmem((cols, near, block, LANES), f32),
            vmem((turns, nx, block, LANES), f32),
            vmem((far, block, LANES), f32),
            vmem((cols, block, LANES), f32),
            vmem((width, LANES), f32),
            vmem((block, width * cols), f32),
            dma((3,)), dma((far,)), dma((far,)), dma((2, near)), dma((2, near)), dma((near,)), dma((near,)),
            dma((far,)), dma((far,)), dma((near,)), dma((near,)), dma((cols,)), dma((cols,)),
            dma((turns, nx)), dma((far,)), dma((cols,)), dma((cols,)), dma((2,)),
        ],
        compiler_params=pltpu.CompilerParams(
            collective_id=0, has_side_effects=True, vmem_limit_bytes=60 * 1024 * 1024
        ),
        cost_estimate=pl.CostEstimate(flops=1 << 30, bytes_accessed=1 << 20, transcendentals=0),
    )(panel, signs.reshape(groups, LANES), sample_rows.reshape(1, LANES))


def build(mesh, dims):
    return jax.shard_map(
        functools.partial(per_device, dims),
        mesh=mesh,
        in_specs=(P("col", "row"), P("row"), P("row")),
        out_specs=(P("col", "row"), P("row", None)),
        check_vma=False,
    )


def solution(mesh):
    return build(mesh, (4, 16, 4, 2))
```
